32 devices in a mesh: row: 2 (over y), col: 4 (over x, core), layer: 4 (over z).
Axes of the slice: x: 2, y: 2, z: 4, core: 2. Of those that a mesh axis runs over, the one named last changes fastest.
Arguments:
- coeffs: float32 [4096, 4096], P(('row', 'col'), 'layer'), may hold values from -6 to 6
- hblocks: float32 [256, 128, 128], P('layer'), may hold values from -0.1875 to 0.1875
- hcount: int32 [32], replicated, may hold values from 1 to 16, 256 in all
- hcols: int32 [256], P('layer'), may hold values from 0 to 31
Outputs:
- sigma: float32 [4096, 4096], P(('row', 'col'), 'layer')
The draws below stay inside these ranges and needn't reach their ends.
Inputs may be any that keep to these rules, and one draw needn't show every extreme that they name: `hcount`: the blocks of a row stand together in hcols and hblocks, rows in order; the counts sum to 256 and some row holds 16. `hcols`: a row may name a column more than once; such blocks add.
All inputs are finite; a program needn't handle non-finite values.
Results may differ from the reference program's by a relative error of at most 0.00007.
Values sent between devices are 32-bit elements; how exact they have to be, the bound alone decides.
A program may use at most 128 MiB of HBM per device.

```python
import math
import jax
import jax.numpy as jnp
import numpy as np
from jax import lax

NSTR = 4096
BLK = 128
NBLK = 32
NZ = 256
MOST = 16


def set_ends(entries, own_key, least, top_value):
    spot = [jax.random.randint(jax.random.fold_in(own_key, axis), (), 0, length) for axis, length in enumerate(entries.shape)]
    main_axis = entries.shape.index(max(entries.shape))
    beside = spot[:main_axis] + [(spot[main_axis] + 1) % entries.shape[main_axis]] + spot[main_axis + 1:]
    return entries.at[tuple(spot)].set(least).at[tuple(beside)].set(top_value)


def shard_levels(own_key, shape, split, low, top_value):
    loudness = 1.0
    for axis_at, parts in split:
        draws = jax.random.uniform(jax.random.fold_in(jax.random.fold_in(own_key, 6), axis_at), (parts,), jnp.float32, low / len(split), top_value / len(split))
        loudness = loudness * jnp.repeat(jnp.exp(draws), shape[axis_at] // parts).reshape((-1,) + (1,) * (len(shape) - 1 - axis_at))
    return loudness


def profile(number_of, total, reach, lean):
    weights = [(1 << 20) // math.isqrt(rank ** lean) + 1 for rank in range(2, number_of + 1)]
    surplus, given = total - reach - (number_of - 1), [1] * (number_of - 1)
    while surplus > 0:
        movable = [i for i in range(number_of - 1) if given[i] < reach]
        whole, remaining = sum([weights[i] for i in movable]), surplus
        for i in movable:
            more = min(reach - given[i], max(1, remaining * weights[i] // whole), surplus)
            given[i] = given[i] + more
            surplus = surplus - more
    return np.array([reach] + given)


def ragged(own_key, number_of, total, reach, skew):
    if number_of == 2:
        one = jax.random.randint(own_key, (), max(1, total - reach), min(reach, total - 1) + 1)
        return jnp.stack([one, total - one])
    lengths = jnp.asarray(profile(number_of, total, reach, skew), jnp.int32)
    pairs = (number_of - 1) // 2
    donor, sink = lengths[1:1 + 2 * pairs:2], lengths[2:2 + 2 * pairs:2]
    margin = jnp.minimum(donor - 1, reach - sink)
    moved = jax.random.randint(jax.random.fold_in(own_key, 1), (pairs,), 0, 1 << 20) % (margin + 1)
    lengths = lengths.at[1:1 + 2 * pairs:2].set(donor - moved).at[2:2 + 2 * pairs:2].set(sink + moved)
    return lengths[jax.random.permutation(jax.random.fold_in(own_key, 2), number_of)]


def centred(rng, dims, scale, bound, shards=(), kind=jnp.bfloat16):
    entries = jax.random.normal(rng, dims, jnp.float32) * scale
    if len(shards) > 0:
        entries = shard_levels(rng, dims, shards, -0.22, 0.18) * entries
    return jnp.clip(entries, min=-bound, max=bound).astype(kind)


def setup_inputs(seed: int = 0) -> dict:
    key_list = jax.random.split(jax.random.key(seed), 5)
    coeffs = centred(key_list[0], (NSTR, NSTR), 1.0, 6.0, ((0, 8), (1, 4)), jnp.float32)
    hblocks = centred(key_list[1], (NZ, BLK, BLK), (BLK * NZ // NBLK) ** -0.5, 0.1875, ((0, 4),), jnp.float32)
    hcount = ragged(key_list[2], NBLK, NZ, MOST, 2).astype(jnp.int32)
    hcols = set_ends(jax.random.randint(key_list[3], (NZ,), 0, NBLK), jax.random.fold_in(key_list[3], 1), 0, NBLK - 1).astype(jnp.int32)
    return dict(coeffs=coeffs, hblocks=hblocks, hcount=hcount, hcols=hcols)


def reference(coeffs, hblocks, hcount, hcols):
    row_end = jnp.cumsum(hcount).astype(jnp.int32)
    stored = jnp.arange(NZ, dtype=jnp.int32)
    owners = jnp.sum((row_end[None, :] <= stored[:, None]).astype(jnp.int32), axis=1).astype(jnp.int32)
    tiled = jnp.zeros((NBLK, NBLK, BLK, BLK), jnp.float32).at[owners, hcols].add(hblocks)
    hamiltonian = tiled.transpose(0, 2, 1, 3).reshape(NSTR, NSTR)
    beta_side = jnp.dot(coeffs, hamiltonian.T, precision=lax.Precision.HIGHEST, preferred_element_type=jnp.float32)
    alpha_side = jnp.dot(hamiltonian, coeffs, precision=lax.Precision.HIGHEST, preferred_element_type=jnp.float32)
    return beta_side + alpha_side
```

```python
import functools

import jax
import jax.numpy as jnp
from jax import lax
from jax.experimental import pallas as pl
from jax.experimental.pallas import tpu as pltpu
from jax.sharding import PartitionSpec as P

MESH = pl.DeviceIdType.MESH
ANY = pl.BlockSpec(memory_space=pl.ANY)


def place():
    return lax.axis_index("row"), lax.axis_index("col"), lax.axis_index("layer")


def plane_peer(sizes, row, col, offset):
    rows, cols, _ = sizes
    down, right = offset // cols, offset % cols
    to = (lax.rem(row + down, rows), lax.rem(col + right, cols))
    source = lax.rem(row + rows - down, rows) * cols + lax.rem(col + cols - right, cols)
    return to, source


def greet(sizes):
    rows, cols, layers = sizes
    row, col, layer = place()
    barrier = pltpu.get_barrier_semaphore()
    for k in range(1, layers):
        to = (row, col, lax.rem(layer + k, layers))
        pl.semaphore_signal(barrier, inc=1, device_id=to, device_id_type=MESH)
    for offset in range(1, rows * cols):
        to, _ = plane_peer(sizes, row, col, offset)
        pl.semaphore_signal(barrier, inc=1, device_id=(*to, layer), device_id_type=MESH)
    pl.semaphore_wait(barrier, layers - 1 + rows * cols - 1)


def remote(src, dst, send_sem, recv_sem, to):
    return pltpu.make_async_remote_copy(
        src_ref=src,
        dst_ref=dst,
        send_sem=send_sem,
        recv_sem=recv_sem,
        device_id=to,
        device_id_type=MESH,
    )


def exchange(sizes, by_layer, by_plane, to_layer, to_plane, sems):
    rows, cols, layers = sizes
    row, col, layer = place()
    layer_send, layer_recv, plane_send, plane_recv = sems
    over_layer, over_plane = [], []
    for k in range(1, layers):
        other = lax.rem(layer + k, layers)
        over_layer.append(
            remote(
                by_layer.at[other],
                to_layer.at[layer],
                layer_send.at[k],
                layer_recv.at[k],
                (row, col, other),
            )
        )
    me = row * cols + col
    for offset in range(1, rows * cols):
        to, _ = plane_peer(sizes, row, col, offset)
        over_plane.append(
            remote(
                by_plane.at[to[0] * cols + to[1]],
                to_plane.at[me],
                plane_send.at[offset],
                plane_recv.at[offset],
                (*to, layer),
            )
        )
    return over_layer, over_plane


def out_kernel(
    sizes,
    c_ref,
    t_ref,
    h_ref,
    k_ref,
    z_ref,
    x_ref,
    all_ref,
    cols_ref,
    own_sem,
    layer_send,
    layer_recv,
    plane_send,
    plane_recv,
    cols_send,
    cols_recv,
    rise_send,
    fall_send,
    relay_recv,
    chip_send,
    chip_recv,
    pair_send,
    pair_recv,
):
    rows, cols, layers = sizes
    row, col, layer = place()
    me = row * cols + col
    step = 2 if cols % 2 == 0 else 1
    offsets = [d * cols + e for d in range(rows) for e in range(0, cols, step)]

    greet(sizes)

    def relay(piece, up):
        src = h_ref.at[me] if piece is None else all_ref.at[piece, me]
        piece = layer if piece is None else piece
        sem = rise_send if up else fall_send
        to = (row, col, layer + 1 if up else layer - 1)
        return remote(src, all_ref.at[piece, me], sem.at[piece], relay_recv.at[piece], to)

    def to_chips(piece):
        made = []
        for at, offset in enumerate(offsets[1:]):
            to, _ = plane_peer(sizes, row, col, offset)
            made.append(
                remote(
                    all_ref.at[piece, me],
                    all_ref.at[piece, me],
                    chip_send.at[piece, at],
                    chip_recv.at[piece, at],
                    (*to, layer),
                )
            )
        return made

    def to_pair(piece, at):
        _, source = plane_peer(sizes, row, col, offsets[at])
        twin = (row, col + 1 - 2 * lax.rem(col, 2), layer)
        return remote(
            all_ref.at[piece, source],
            all_ref.at[piece, source],
            pair_send.at[piece, at],
            pair_recv.at[piece, at],
            twin,
        )

    def each_piece(k, act):
        @pl.when(layer >= k)
        def below():
            act(layer - k, True)

        @pl.when(layer + k < layers)
        def above():
            act(layer + k, False)

    can_rise, can_fall = layer + 1 < layers, layer > 0

    @pl.when(can_rise)
    def rise():
        relay(None, True).start()

    @pl.when(can_fall)
    def fall():
        relay(None, False).start()

    over_layer, over_plane = exchange(
        sizes, c_ref, t_ref, z_ref, x_ref, (layer_send, layer_recv, plane_send, plane_recv)
    )
    names = []
    for k in range(1, layers):
        to = (row, col, lax.rem(layer + k, layers))
        names.append(remote(k_ref, cols_ref.at[layer], cols_send.at[k], cols_recv.at[k], to))
    own = [
        pltpu.make_async_copy(c_ref.at[layer], z_ref.at[layer], own_sem.at[0]),
        pltpu.make_async_copy(t_ref.at[me], x_ref.at[me], own_sem.at[1]),
        pltpu.make_async_copy(h_ref, all_ref.at[layer], own_sem.at[2]),
        pltpu.make_async_copy(k_ref, cols_ref.at[layer], own_sem.at[3]),
    ]
    for copy in names + over_plane + own:
        copy.start()

    def arrive(piece, upward):
        relay(piece, upward).wait_recv()

        @pl.when(can_rise if upward else can_fall)
        def onward():
            relay(piece, upward).start()

        for copy in to_chips(piece):
            copy.start()
        if step == 2:
            to_pair(piece, 0).start()

    late = min(2, layers - 1)
    for k in range(1, layers):
        each_piece(k, arrive)
        if k == late:
            for copy in over_layer:
                copy.start()
    if layers == 1:
        for copy in over_layer:
            copy.start()

    def pass_on(piece, upward):
        for at, copy in enumerate(to_chips(piece)):
            copy.wait_recv()
            if step == 2:
                to_pair(piece, at + 1).start()

    for k in range(1, layers):
        each_piece(k, pass_on)

    def finish(piece, upward):
        @pl.when(can_rise if upward else can_fall)
        def sent():
            relay(piece, upward).wait_send()

        for copy in to_chips(piece):
            copy.wait_send()
        if step == 2:
            for at in range(len(offsets)):
                copy = to_pair(piece, at)
                copy.wait_send()
                copy.wait_recv()

    for k in range(1, layers):
        each_piece(k, finish)

    @pl.when(can_rise)
    def risen():
        relay(None, True).wait_send()

    @pl.when(can_fall)
    def fallen():
        relay(None, False).wait_send()

    for copy in names + over_plane + over_layer + own:
        copy.wait()


def back_kernel(
    sizes,
    b_ref,
    a_ref,
    beta_ref,
    alpha_ref,
    own_sem,
    layer_send,
    layer_recv,
    plane_send,
    plane_recv,
):
    rows, cols, layers = sizes
    row, col, layer = place()
    me = row * cols + col
    greet(sizes)
    over_layer, over_plane = exchange(
        sizes, b_ref, a_ref, beta_ref, alpha_ref, (layer_send, layer_recv, plane_send, plane_recv)
    )
    own = [
        pltpu.make_async_copy(b_ref.at[layer], beta_ref.at[layer], own_sem.at[0]),
        pltpu.make_async_copy(a_ref.at[me], alpha_ref.at[me], own_sem.at[1]),
    ]
    for copy in over_layer + over_plane + own:
        copy.start()
    for copy in over_layer + over_plane + own:
        copy.wait()


def halves(values):
    high = values.astype(jnp.bfloat16)
    low = (values - high.astype(jnp.float32)).astype(jnp.bfloat16)
    return high, low


def product_kernel(owner_ref, column_ref, z_ref, x_ref, h_ref, a_ref, b_ref, y_ref):
    chunk, block = h_ref.shape[0], h_ref.shape[1]
    blocks, alpha_rows, _ = a_ref.shape
    step = pl.program_id(0)

    @pl.when(step == 0)
    def prepare():
        a_ref[...] = jnp.zeros_like(a_ref)
        b_ref[...] = jnp.zeros_like(b_ref)
        for ref, low_row in ((x_ref, 0), (z_ref, alpha_rows)):
            per = ref.shape[2] // block
            count = ref.shape[1]
            for j in range(blocks):
                part = ref[j // per, :, (j % per) * block : (j % per + 1) * block]
                high, low = halves(part)
                y_ref[j, low_row : low_row + count, :block] = high
                y_ref[j, low_row : low_row + count, block:] = low

    group = 4

    def body(at, carry):
        results = []
        for i in range(group):
            n = at * group + i
            high, low = halves(h_ref[n])
            weights = jnp.concatenate(
                [jnp.concatenate([high, high], axis=1), jnp.concatenate([low, low], axis=1)], axis=0
            )
            picked = y_ref[column_ref[step * chunk + n]]
            both = lax.dot_general(
                picked, weights, (((1,), (1,)), ((), ())), preferred_element_type=jnp.float32
            )
            results.append(both[:, :block] + both[:, block:])
        for i in range(group):
            owner = owner_ref[step * chunk + at * group + i]
            a_ref[owner] += results[i][:alpha_rows]
            b_ref[owner] += results[i][alpha_rows:]
        return carry

    lax.fori_loop(0, chunk // group, body, 0)


def local(sizes, coeffs, hblocks, hcount, hcols):
    rows, cols, layers = sizes
    group = rows * cols
    row_count, col_count = coeffs.shape
    share, block, _ = hblocks.shape
    stored = share * layers
    blocks = row_count * group // block
    alpha_rows, beta_rows = col_count // group, row_count // layers
    f32 = jnp.float32
    dma = pltpu.SemaphoreType.DMA

    padded = -(-share // 1024) * 1024
    names = jnp.pad(hcols, (0, padded - share)).reshape(-1, 128)
    flipped = coeffs.T.reshape(group, alpha_rows, row_count)
    chips = group // 2 if cols % 2 == 0 else group
    z, x, everything, columns = pl.pallas_call(
        functools.partial(out_kernel, sizes),
        out_shape=(
            jax.ShapeDtypeStruct((layers, beta_rows, col_count), f32),
            jax.ShapeDtypeStruct((group, alpha_rows, row_count), f32),
            jax.ShapeDtypeStruct((layers, group, share // group, block, block), f32),
            jax.ShapeDtypeStruct((layers, *names.shape), jnp.int32),
        ),
        in_specs=[ANY] * 4,
        out_specs=(ANY,) * 4,
        scratch_shapes=[dma((4,))]
        + [dma((layers,))] * 2
        + [dma((group,))] * 2
        + [dma((layers,))] * 5
        + [dma((layers, chips))] * 4,
        compiler_params=pltpu.CompilerParams(collective_id=0, has_side_effects=True),
        name="spread",
    )(
        coeffs.reshape(layers, beta_rows, col_count),
        flipped,
        hblocks.reshape(group, share // group, block, block),
        names,
    )

    row_end = jnp.cumsum(hcount)
    index = jnp.arange(stored, dtype=jnp.int32)
    owners = jnp.sum((row_end[None, :] <= index[:, None]).astype(jnp.int32), axis=1)
    columns = columns.reshape(layers, -1)[:, :share].reshape(stored)
    chunk = 16
    whole = lambda shape: pl.BlockSpec(shape, lambda i, *_: (0,) * len(shape))
    a_shape, b_shape = (blocks, alpha_rows, block), (blocks, beta_rows, block)
    alpha, beta = pl.pallas_call(
        product_kernel,
        out_shape=(jax.ShapeDtypeStruct(a_shape, f32), jax.ShapeDtypeStruct(b_shape, f32)),
        grid_spec=pltpu.PrefetchScalarGridSpec(
            num_scalar_prefetch=2,
            grid=(stored // chunk,),
            in_specs=[
                whole(z.shape),
                whole(x.shape),
                pl.BlockSpec((chunk, block, block), lambda i, *_: (i, 0, 0)),
            ],
            out_specs=(whole(a_shape), whole(b_shape)),
            scratch_shapes=[pltpu.VMEM((blocks, alpha_rows + beta_rows, 2 * block), jnp.bfloat16)],
        ),
        compiler_params=pltpu.CompilerParams(vmem_limit_bytes=48 * 2**20),
        name="product",
    )(owners, columns, z, x, everything.reshape(stored, block, block))

    per_layer, per_plane = blocks // layers, blocks // group
    beta_back = (layers, per_layer, beta_rows, block)
    alpha_back = (group, per_plane, alpha_rows, block)
    beta, alpha = pl.pallas_call(
        functools.partial(back_kernel, sizes),
        out_shape=(jax.ShapeDtypeStruct(beta_back, f32), jax.ShapeDtypeStruct(alpha_back, f32)),
        in_specs=[ANY] * 2,
        out_specs=(ANY,) * 2,
        scratch_shapes=[dma((2,))] + [dma((layers,))] * 2 + [dma((group,))] * 2,
        compiler_params=pltpu.CompilerParams(collective_id=1, has_side_effects=True),
        name="collect",
    )(beta.reshape(beta_back), alpha.reshape(alpha_back))
    beta = beta.transpose(0, 2, 1, 3).reshape(row_count, col_count)
    alpha = alpha.transpose(1, 3, 0, 2).reshape(row_count, col_count)
    return beta + alpha


def solution(mesh):
    sizes = tuple(mesh.shape[name] for name in ("row", "col", "layer"))
    in_specs = (P(("row", "col"), "layer"), P("layer", None, None), P(), P("layer"))
    out_specs = P(("row", "col"), "layer")
    return jax.shard_map(
        functools.partial(local, sizes),
        mesh=mesh,
        in_specs=in_specs,
        out_specs=out_specs,
        check_vma=False,
    )
```

```python
import functools

import jax
import jax.numpy as jnp
from jax import lax
from jax.experimental import pallas as pl
from jax.experimental.pallas import tpu as pltpu
from jax.sharding import PartitionSpec as P

MESH = pl.DeviceIdType.MESH
ANY = pl.BlockSpec(memory_space=pl.ANY)


def place():
    return lax.axis_index("row"), lax.axis_index("col"), lax.axis_index("layer")


def plane_peer(sizes, row, col, offset):
    rows, cols, _ = sizes
    down, right = offset // cols, offset % cols
    to = (lax.rem(row + down, rows), lax.rem(col + right, cols))
    source = lax.rem(row + rows - down, rows) * cols + lax.rem(col + cols - right, cols)
    return to, source


def greet(sizes):
    rows, cols, layers = sizes
    row, col, layer = place()
    barrier = pltpu.get_barrier_semaphore()
    for k in range(1, layers):
        to = (row, col, lax.rem(layer + k, layers))
        pl.semaphore_signal(barrier, inc=1, device_id=to, device_id_type=MESH)
    for offset in range(1, rows * cols):
        to, _ = plane_peer(sizes, row, col, offset)
        pl.semaphore_signal(barrier, inc=1, device_id=(*to, layer), device_id_type=MESH)
    pl.semaphore_wait(barrier, layers - 1 + rows * cols - 1)


def remote(src, dst, send_sem, recv_sem, to):
    return pltpu.make_async_remote_copy(
        src_ref=src,
        dst_ref=dst,
        send_sem=send_sem,
        recv_sem=recv_sem,
        device_id=to,
        device_id_type=MESH,
    )


def exchange(sizes, by_layer, by_plane, to_layer, to_plane, sems):
    rows, cols, layers = sizes
    row, col, layer = place()
    layer_send, layer_recv, plane_send, plane_recv = sems
    over_layer, over_plane = [], []
    for k in range(1, layers):
        other = lax.rem(layer + k, layers)
        over_layer.append(
            remote(
                by_layer.at[other],
                to_layer.at[layer],
                layer_send.at[k],
                layer_recv.at[k],
                (row, col, other),
            )
        )
    me = row * cols + col
    for offset in range(1, rows * cols):
        to, _ = plane_peer(sizes, row, col, offset)
        over_plane.append(
            remote(
                by_plane.at[to[0] * cols + to[1]],
                to_plane.at[me],
                plane_send.at[offset],
                plane_recv.at[offset],
                (*to, layer),
            )
        )
    return over_layer, over_plane


def out_kernel(
    sizes,
    c_ref,
    t_ref,
    h_ref,
    k_ref,
    z_ref,
    x_ref,
    all_ref,
    cols_ref,
    own_sem,
    layer_send,
    layer_recv,
    plane_send,
    plane_recv,
    cols_send,
    cols_recv,
    rise_send,
    fall_send,
    relay_recv,
    chip_send,
    chip_recv,
    pair_send,
    pair_recv,
):
    rows, cols, layers = sizes
    row, col, layer = place()
    me = row * cols + col
    step = 2 if cols % 2 == 0 else 1
    offsets = [d * cols + e for d in range(rows) for e in range(0, cols, step)]
    half = h_ref.shape[1] // 2
    square = rows == 2 and cols == 4 and half > 0

    greet(sizes)

    def relay(piece, up):
        src = h_ref.at[me] if piece is None else all_ref.at[piece, me]
        piece = layer if piece is None else piece
        sem = rise_send if up else fall_send
        to = (row, col, layer + 1 if up else layer - 1)
        return remote(src, all_ref.at[piece, me], sem.at[piece], relay_recv.at[piece], to)

    def to_chip(piece, at):
        to, _ = plane_peer(sizes, row, col, offsets[at])
        return remote(
            all_ref.at[piece, me],
            all_ref.at[piece, me],
            chip_send.at[piece, at],
            chip_recv.at[piece, at],
            (*to, layer),
        )

    def to_corner(piece, part):
        _, source = plane_peer(sizes, row, col, offsets[1 + part])
        to, _ = plane_peer(sizes, row, col, offsets[2 - part])
        block = all_ref.at[piece, source, pl.ds(part * half, half)]
        at = 0 if part == 0 else 3
        return remote(block, block, chip_send.at[piece, at], chip_recv.at[piece, at], (*to, layer))

    def to_pair(piece, at):
        _, source = plane_peer(sizes, row, col, offsets[at])
        twin = (row, col + 1 - 2 * lax.rem(col, 2), layer)
        return remote(
            all_ref.at[piece, source],
            all_ref.at[piece, source],
            pair_send.at[piece, at],
            pair_recv.at[piece, at],
            twin,
        )

    chips = [1, 2] if square else list(range(1, len(offsets)))

    def each_piece(k, act):
        @pl.when(layer >= k)
        def below():
            act(layer - k, True)

        @pl.when(layer + k < layers)
        def above():
            act(layer + k, False)

    can_rise, can_fall = layer + 1 < layers, layer > 0

    @pl.when(can_rise)
    def rise():
        relay(None, True).start()

    @pl.when(can_fall)
    def fall():
        relay(None, False).start()

    over_layer, over_plane = exchange(
        sizes, c_ref, t_ref, z_ref, x_ref, (layer_send, layer_recv, plane_send, plane_recv)
    )
    names = []
    for k in range(1, layers):
        to = (row, col, lax.rem(layer + k, layers))
        names.append(remote(k_ref, cols_ref.at[layer], cols_send.at[k], cols_recv.at[k], to))
    own = [
        pltpu.make_async_copy(c_ref.at[layer], z_ref.at[layer], own_sem.at[0]),
        pltpu.make_async_copy(t_ref.at[me], x_ref.at[me], own_sem.at[1]),
        pltpu.make_async_copy(k_ref, cols_ref.at[layer], own_sem.at[2]),
    ]
    for copy in names + over_plane + own:
        copy.start()

    def arrive(piece, upward):
        relay(piece, upward).wait_recv()

        @pl.when(can_rise if upward else can_fall)
        def onward():
            relay(piece, upward).start()

        for at in chips:
            to_chip(piece, at).start()
        if step == 2:
            to_pair(piece, 0).start()

    def pass_on(piece, upward):
        for at in chips:
            to_chip(piece, at).wait_recv()
            if square:
                to_corner(piece, at - 1).start()
            if step == 2:
                to_pair(piece, at).start()

    def pass_corner(piece, upward):
        if square:
            to_corner(piece, 0).wait_recv()
            to_corner(piece, 1).wait_recv()
            to_pair(piece, 3).start()

    for k in range(1, layers):
        each_piece(k, arrive)
        if k > 1 and k < layers - 1:
            each_piece(k - 1, pass_on)
    for copy in over_layer:
        copy.start()
    if layers > 2:
        each_piece(layers - 2, pass_on)
        each_piece(1, pass_corner) if layers > 3 else None
    if layers > 1:
        each_piece(layers - 1, pass_on)
    for k in range(2 if layers > 3 else 1, layers):
        each_piece(k, pass_corner)

    def finish(piece, upward):
        @pl.when(can_rise if upward else can_fall)
        def sent():
            relay(piece, upward).wait_send()

        for at in chips:
            to_chip(piece, at).wait_send()
        if square:
            to_corner(piece, 0).wait_send()
            to_corner(piece, 1).wait_send()
        if step == 2:
            for at in range(len(offsets)):
                copy = to_pair(piece, at)
                copy.wait_send()
                copy.wait_recv()

    for k in range(1, layers):
        each_piece(k, finish)

    @pl.when(can_rise)
    def risen():
        relay(None, True).wait_send()

    @pl.when(can_fall)
    def fallen():
        relay(None, False).wait_send()

    for copy in names + over_plane + over_layer + own:
        copy.wait()


def back_kernel(
    sizes,
    b_ref,
    a_ref,
    beta_ref,
    alpha_ref,
    own_sem,
    layer_send,
    layer_recv,
    plane_send,
    plane_recv,
):
    rows, cols, layers = sizes
    row, col, layer = place()
    me = row * cols + col
    greet(sizes)
    over_layer, over_plane = exchange(
        sizes, b_ref, a_ref, beta_ref, alpha_ref, (layer_send, layer_recv, plane_send, plane_recv)
    )
    own = [
        pltpu.make_async_copy(b_ref.at[layer], beta_ref.at[layer], own_sem.at[0]),
        pltpu.make_async_copy(a_ref.at[me], alpha_ref.at[me], own_sem.at[1]),
    ]
    for copy in over_layer + over_plane + own:
        copy.start()
    for copy in over_layer + over_plane + own:
        copy.wait()


def halves(values):
    high = values.astype(jnp.bfloat16)
    low = (values - high.astype(jnp.float32)).astype(jnp.bfloat16)
    return high, low


def product_kernel(
    own_steps, owner_ref, column_ref, first_ref, z_ref, x_ref, own_ref, h_ref, a_ref, b_ref, y_ref
):
    chunk, block = h_ref.shape[0], h_ref.shape[1]
    stored = owner_ref.shape[0]
    blocks, alpha_rows, _ = a_ref.shape
    step = pl.program_id(0)

    @pl.when(step == 0)
    def prepare():
        a_ref[...] = jnp.zeros_like(a_ref)
        b_ref[...] = jnp.zeros_like(b_ref)
        for ref, low_row in ((x_ref, 0), (z_ref, alpha_rows)):
            per = ref.shape[2] // block
            count = ref.shape[1]
            for j in range(blocks):
                part = ref[j // per, :, (j % per) * block : (j % per + 1) * block]
                high, low = halves(part)
                y_ref[j, low_row : low_row + count, :block] = high
                y_ref[j, low_row : low_row + count, block:] = low

    start = lax.rem(first_ref[0] + step * chunk, stored)
    group = 4

    def run(ref):
        def body(at, carry):
            results = []
            for i in range(group):
                n = at * group + i
                high, low = halves(ref[n])
                weights = jnp.concatenate(
                    [
                        jnp.concatenate([high, high], axis=1),
                        jnp.concatenate([low, low], axis=1),
                    ],
                    axis=0,
                )
                picked = y_ref[column_ref[start + n]]
                both = lax.dot_general(
                    picked, weights, (((1,), (1,)), ((), ())), preferred_element_type=jnp.float32
                )
                results.append(both[:, :block] + both[:, block:])
            for i in range(group):
                owner = owner_ref[start + at * group + i]
                a_ref[owner] += results[i][:alpha_rows]
                b_ref[owner] += results[i][alpha_rows:]
            return carry

        lax.fori_loop(0, chunk // group, body, 0)

    pl.when(step < own_steps)(lambda: run(own_ref))
    pl.when(step >= own_steps)(lambda: run(h_ref))


def join_kernel(b_ref, a_ref, out_ref):
    block = b_ref.shape[-1]
    for p in range(b_ref.shape[1]):
        out_ref[:, p * block : (p + 1) * block] = b_ref[0, p] + a_ref[p, 0].T


def local(sizes, coeffs, hblocks, hcount, hcols):
    rows, cols, layers = sizes
    group = rows * cols
    row_count, col_count = coeffs.shape
    share, block, _ = hblocks.shape
    stored = share * layers
    blocks = row_count * group // block
    alpha_rows, beta_rows = col_count // group, row_count // layers
    f32 = jnp.float32
    dma = pltpu.SemaphoreType.DMA

    padded = -(-share // 1024) * 1024
    names = jnp.pad(hcols, (0, padded - share)).reshape(-1, 128)
    flipped = coeffs.T.reshape(group, alpha_rows, row_count)
    chips = group // 2 if cols % 2 == 0 else group
    z, x, everything, columns = pl.pallas_call(
        functools.partial(out_kernel, sizes),
        out_shape=(
            jax.ShapeDtypeStruct((layers, beta_rows, col_count), f32),
            jax.ShapeDtypeStruct((group, alpha_rows, row_count), f32),
            jax.ShapeDtypeStruct((layers, group, share // group, block, block), f32),
            jax.ShapeDtypeStruct((layers, *names.shape), jnp.int32),
        ),
        in_specs=[ANY] * 4,
        out_specs=(ANY,) * 4,
        scratch_shapes=[dma((3,))]
        + [dma((layers,))] * 2
        + [dma((group,))] * 2
        + [dma((layers,))] * 5
        + [dma((layers, chips))] * 4,
        compiler_params=pltpu.CompilerParams(collective_id=0, has_side_effects=True),
        name="spread",
    )(
        coeffs.reshape(layers, beta_rows, col_count),
        flipped,
        hblocks.reshape(group, share // group, block, block),
        names,
    )

    row_end = jnp.cumsum(hcount)
    index = jnp.arange(stored, dtype=jnp.int32)
    owners = jnp.sum((row_end[None, :] <= index[:, None]).astype(jnp.int32), axis=1)
    columns = columns.reshape(layers, -1)[:, :share].reshape(stored)
    chunk = 16
    own_steps, steps = share // chunk, stored // chunk
    first = jnp.reshape(lax.axis_index("layer") * share, (1,)).astype(jnp.int32)
    whole = lambda shape: pl.BlockSpec(shape, lambda i, *_: (0,) * len(shape))

    def own_at(i, owner_ref, column_ref, first_ref):
        return jnp.minimum(i, own_steps - 1), 0, 0

    def other_at(i, owner_ref, column_ref, first_ref):
        later = jnp.maximum(i, min(own_steps, steps - 1))
        return lax.rem(first_ref[0] // chunk + later, steps), 0, 0

    a_shape, b_shape = (blocks, alpha_rows, block), (blocks, beta_rows, block)
    alpha, beta = pl.pallas_call(
        functools.partial(product_kernel, own_steps),
        out_shape=(jax.ShapeDtypeStruct(a_shape, f32), jax.ShapeDtypeStruct(b_shape, f32)),
        grid_spec=pltpu.PrefetchScalarGridSpec(
            num_scalar_prefetch=3,
            grid=(steps,),
            in_specs=[
                whole(z.shape),
                whole(x.shape),
                pl.BlockSpec((chunk, block, block), own_at),
                pl.BlockSpec((chunk, block, block), other_at),
            ],
            out_specs=(whole(a_shape), whole(b_shape)),
            scratch_shapes=[pltpu.VMEM((blocks, alpha_rows + beta_rows, 2 * block), jnp.bfloat16)],
        ),
        compiler_params=pltpu.CompilerParams(vmem_limit_bytes=48 * 2**20),
        name="product",
    )(owners, columns, first, z, x, hblocks, everything.reshape(stored, block, block))

    per_layer, per_plane = blocks // layers, blocks // group
    beta_back = (layers, per_layer, beta_rows, block)
    alpha_back = (group, per_plane, alpha_rows, block)
    beta, alpha = pl.pallas_call(
        functools.partial(back_kernel, sizes),
        out_shape=(jax.ShapeDtypeStruct(beta_back, f32), jax.ShapeDtypeStruct(alpha_back, f32)),
        in_specs=[ANY] * 2,
        out_specs=(ANY,) * 2,
        scratch_shapes=[dma((2,))] + [dma((layers,))] * 2 + [dma((group,))] * 2,
        compiler_params=pltpu.CompilerParams(collective_id=1, has_side_effects=True),
        name="collect",
    )(beta.reshape(beta_back), alpha.reshape(alpha_back))
    if alpha_rows == block and beta_rows == block:
        return pl.pallas_call(
            join_kernel,
            out_shape=jax.ShapeDtypeStruct((row_count, col_count), f32),
            grid=(layers,),
            in_specs=[
                pl.BlockSpec((1, per_layer, block, block), lambda i: (i, 0, 0, 0)),
                pl.BlockSpec((group, 1, block, block), lambda i: (0, i, 0, 0)),
            ],
            out_specs=pl.BlockSpec((block, col_count), lambda i: (i, 0)),
            name="join",
        )(beta, alpha)
    beta = beta.transpose(0, 2, 1, 3).reshape(row_count, col_count)
    alpha = alpha.transpose(1, 3, 0, 2).reshape(row_count, col_count)
    return beta + alpha


def solution(mesh):
    sizes = tuple(mesh.shape[name] for name in ("row", "col", "layer"))
    in_specs = (P(("row", "col"), "layer"), P("layer", None, None), P(), P("layer"))
    out_specs = P(("row", "col"), "layer")
    return jax.shard_map(
        functools.partial(local, sizes),
        mesh=mesh,
        in_specs=in_specs,
        out_specs=out_specs,
        check_vma=False,
    )
```

```python
import functools

import jax
import jax.numpy as jnp
from jax import lax
from jax.experimental import pallas as pl
from jax.experimental.pallas import tpu as pltpu
from jax.sharding import PartitionSpec as P

MESH = pl.DeviceIdType.MESH
ANY = pl.BlockSpec(memory_space=pl.ANY)


def place():
    return lax.axis_index("row"), lax.axis_index("col"), lax.axis_index("layer")


def plane_peer(sizes, row, col, offset):
    rows, cols, _ = sizes
    down, right = offset // cols, offset % cols
    to = (lax.rem(row + down, rows), lax.rem(col + right, cols))
    source = lax.rem(row + rows - down, rows) * cols + lax.rem(col + cols - right, cols)
    return to, source


def greet(sizes):
    rows, cols, layers = sizes
    row, col, layer = place()
    barrier = pltpu.get_barrier_semaphore()
    for k in range(1, layers):
        to = (row, col, lax.rem(layer + k, layers))
        pl.semaphore_signal(barrier, inc=1, device_id=to, device_id_type=MESH)
    for offset in range(1, rows * cols):
        to, _ = plane_peer(sizes, row, col, offset)
        pl.semaphore_signal(barrier, inc=1, device_id=(*to, layer), device_id_type=MESH)
    pl.semaphore_wait(barrier, layers - 1 + rows * cols - 1)


def remote(src, dst, send_sem, recv_sem, to):
    return pltpu.make_async_remote_copy(
        src_ref=src,
        dst_ref=dst,
        send_sem=send_sem,
        recv_sem=recv_sem,
        device_id=to,
        device_id_type=MESH,
    )


def exchange(sizes, by_layer, by_plane, to_layer, to_plane, sems):
    rows, cols, layers = sizes
    row, col, layer = place()
    layer_send, layer_recv, plane_send, plane_recv = sems
    over_layer, over_plane = [], []
    for k in range(1, layers):
        other = lax.rem(layer + k, layers)
        over_layer.append(
            remote(
                by_layer.at[other],
                to_layer.at[layer],
                layer_send.at[k],
                layer_recv.at[k],
                (row, col, other),
            )
        )
    me = row * cols + col
    for offset in range(1, rows * cols):
        to, _ = plane_peer(sizes, row, col, offset)
        over_plane.append(
            remote(
                by_plane.at[to[0] * cols + to[1]],
                to_plane.at[me],
                plane_send.at[offset],
                plane_recv.at[offset],
                (*to, layer),
            )
        )
    return over_layer, over_plane


def halves(values):
    high = values.astype(jnp.bfloat16)
    low = (values - high.astype(jnp.float32)).astype(jnp.bfloat16)
    return high, low


def prepare(z_ref, x_ref, y_ref, block):
    alpha_rows = x_ref.shape[1]
    for ref, low_row in ((x_ref, 0), (z_ref, alpha_rows)):
        per = ref.shape[2] // block
        count = ref.shape[1]
        for j in range(y_ref.shape[0]):
            part = ref[j // per, :, (j % per) * block : (j % per + 1) * block]
            high, low = halves(part)
            y_ref[j, low_row : low_row + count, :block] = high
            y_ref[j, low_row : low_row + count, block:] = low


def multiply(piece, all_ref, names_ref, keep_ref, y_ref, sums_ref):
    _, share, block, _ = all_ref.shape
    group = 8 if share % 8 == 0 else 1

    def body(at, carry):
        results = []
        for i in range(group):
            n = at * group + i
            high, low = halves(all_ref[piece, n])
            weights = jnp.concatenate(
                [jnp.concatenate([high, high], axis=1), jnp.concatenate([low, low], axis=1)], axis=0
            )
            picked = y_ref[names_ref[piece, lax.div(n, 128), lax.rem(n, 128)]]
            both = lax.dot_general(
                picked, weights, (((1,), (1,)), ((), ())), preferred_element_type=jnp.float32
            )
            results.append(both[:, :block] + both[:, block:])
        running = sums_ref[at * group]
        for i in range(group):
            n = at * group + i
            running = results[i] + keep_ref[piece * share + n] * running
            sums_ref[n + 1] = running
        return carry

    lax.fori_loop(0, share // group, body, 0)


def gather(piece, last_ref, found_ref, sums_ref, a_ref, b_ref):
    alpha_rows = a_ref.shape[2]
    per_a, per_b = a_ref.shape[1], b_ref.shape[1]
    blocks = a_ref.shape[0] * per_a

    def body(i, carry):
        part = found_ref[piece * blocks + i] * sums_ref[last_ref[piece * blocks + i]]
        a_ref[lax.div(i, per_a), lax.rem(i, per_a)] += part[:alpha_rows]
        b_ref[lax.div(i, per_b), lax.rem(i, per_b)] += part[alpha_rows:]
        return carry

    lax.fori_loop(0, blocks, body, 0)


def sigma_kernel(
    sizes,
    c_ref,
    t_ref,
    h_ref,
    k_ref,
    keep_ref,
    last_ref,
    found_ref,
    beta_ref,
    alpha_ref,
    cols_ref,
    z_ref,
    x_ref,
    all_ref,
    y_ref,
    sums_ref,
    b_ref,
    a_ref,
    names_ref,
    own_sem,
    back_layer_send,
    back_layer_recv,
    back_plane_send,
    back_plane_recv,
    layer_send,
    layer_recv,
    plane_send,
    plane_recv,
    cols_send,
    cols_recv,
    rise_send,
    fall_send,
    relay_recv,
    chip_send,
    chip_recv,
    pair_send,
    pair_recv,
):
    rows, cols, layers = sizes
    row, col, layer = place()
    me = row * cols + col
    step = 2 if cols % 2 == 0 else 1
    offsets = [d * cols + e for d in range(rows) for e in range(0, cols, step)]
    share, block, _ = h_ref.shape
    size = share // (rows * cols)
    half = size // 2
    square = rows == 2 and cols == 4 and half > 0

    def piece_at(piece, source):
        return all_ref.at[piece, pl.ds(pl.multiple_of(source * size, size), size)]

    greet(sizes)

    def relay(piece, up):
        mine = h_ref.at[pl.ds(pl.multiple_of(me * size, size), size)]
        src = mine if piece is None else piece_at(piece, me)
        piece = layer if piece is None else piece
        sem = rise_send if up else fall_send
        to = (row, col, layer + 1 if up else layer - 1)
        return remote(src, piece_at(piece, me), sem.at[piece], relay_recv.at[piece], to)

    def to_chip(piece, at):
        to, _ = plane_peer(sizes, row, col, offsets[at])
        return remote(
            piece_at(piece, me),
            piece_at(piece, me),
            chip_send.at[piece, at],
            chip_recv.at[piece, at],
            (*to, layer),
        )

    def to_corner(piece, part):
        _, source = plane_peer(sizes, row, col, offsets[1 + part])
        to, _ = plane_peer(sizes, row, col, offsets[2 - part])
        first = pl.multiple_of(source * size + part * half, half)
        part_ref = all_ref.at[piece, pl.ds(first, half)]
        at = 0 if part == 0 else 3
        sems = chip_send.at[piece, at], chip_recv.at[piece, at]
        return remote(part_ref, part_ref, *sems, (*to, layer))

    def to_pair(piece, at):
        _, source = plane_peer(sizes, row, col, offsets[at])
        twin = (row, col + 1 - 2 * lax.rem(col, 2), layer)
        return remote(
            piece_at(piece, source),
            piece_at(piece, source),
            pair_send.at[piece, at],
            pair_recv.at[piece, at],
            twin,
        )

    chips = [1, 2] if square else list(range(1, len(offsets)))

    def each_piece(k, act):
        @pl.when(layer >= k)
        def below():
            act(layer - k, True)

        @pl.when(layer + k < layers)
        def above():
            act(layer + k, False)

    can_rise, can_fall = layer + 1 < layers, layer > 0

    @pl.when(can_rise)
    def rise():
        relay(None, True).start()

    @pl.when(can_fall)
    def fall():
        relay(None, False).start()

    over_layer, over_plane = exchange(
        sizes, c_ref, t_ref, z_ref, x_ref, (layer_send, layer_recv, plane_send, plane_recv)
    )
    names = []
    for k in range(1, layers):
        to = (row, col, lax.rem(layer + k, layers))
        names.append(remote(k_ref, cols_ref.at[layer], cols_send.at[k], cols_recv.at[k], to))
    own = [
        pltpu.make_async_copy(c_ref.at[layer], z_ref.at[layer], own_sem.at[0]),
        pltpu.make_async_copy(t_ref.at[me], x_ref.at[me], own_sem.at[1]),
        pltpu.make_async_copy(k_ref, cols_ref.at[layer], own_sem.at[2]),
        pltpu.make_async_copy(h_ref, all_ref.at[layer], own_sem.at[3]),
    ]
    for copy in names + over_plane + own:
        copy.start()

    def arrive(piece, upward):
        relay(piece, upward).wait_recv()

        @pl.when(can_rise if upward else can_fall)
        def onward():
            relay(piece, upward).start()

        for at in chips:
            to_chip(piece, at).start()
        if step == 2:
            to_pair(piece, 0).start()

    def pass_on(piece, upward):
        for at in chips:
            to_chip(piece, at).wait_recv()
            if square:
                to_corner(piece, at - 1).start()
            if step == 2:
                to_pair(piece, at).start()

    def pass_corner(piece, upward):
        if square:
            to_corner(piece, 0).wait_recv()
            to_corner(piece, 1).wait_recv()
            to_pair(piece, 3).start()

    early = min(2, layers - 1)
    for k in range(1, layers):
        each_piece(k, arrive)
        if k == early:
            for copy in over_layer:
                copy.start()
        if k > 1 and k < layers - 1:
            each_piece(k - 1, pass_on)
    if layers > 2:
        each_piece(layers - 2, pass_on)
    for k in range(1, layers - 2):
        each_piece(k, pass_corner)
    if layers > 1:
        each_piece(layers - 1, pass_on)
    if layers > 2:
        each_piece(layers - 2, pass_corner)

    for copy in names + over_plane + own[:3]:
        copy.wait()
    to_scalars = pltpu.make_async_copy(cols_ref, names_ref, own_sem.at[4])
    to_scalars.start()
    for copy in over_layer:
        copy.wait()
    prepare(z_ref, x_ref, y_ref, block)
    a_ref[...] = jnp.zeros_like(a_ref)
    b_ref[...] = jnp.zeros_like(b_ref)
    sums_ref[0] = jnp.zeros_like(sums_ref[0])
    to_scalars.wait()
    own[3].wait()

    sign = 1 - 2 * lax.div(2 * layer, layers)

    def treat(t, carry):
        piece = lax.rem(layer + layers + t * sign, layers)

        if step == 2:

            @pl.when(t > 0)
            def complete():
                for at in range(len(offsets)):
                    to_pair(piece, at).wait_recv()

        multiply(piece, all_ref, names_ref, keep_ref, y_ref, sums_ref)
        gather(piece, last_ref, found_ref, sums_ref, a_ref, b_ref)

        @pl.when(t == 0)
        def corners():
            if layers > 1:
                each_piece(layers - 1, pass_corner)

        return carry

    lax.fori_loop(0, layers, treat, 0)

    sems = (back_layer_send, back_layer_recv, back_plane_send, back_plane_recv)
    back_layer, back_plane = exchange(sizes, b_ref, a_ref, beta_ref, alpha_ref, sems)
    keep = [
        pltpu.make_async_copy(b_ref.at[layer], beta_ref.at[layer], own_sem.at[5]),
        pltpu.make_async_copy(a_ref.at[me], alpha_ref.at[me], own_sem.at[6]),
    ]
    for copy in back_layer + back_plane + keep:
        copy.start()

    def finish(piece, upward):
        @pl.when(can_rise if upward else can_fall)
        def sent():
            relay(piece, upward).wait_send()

        for at in chips:
            to_chip(piece, at).wait_send()
        if square:
            to_corner(piece, 0).wait_send()
            to_corner(piece, 1).wait_send()
        if step == 2:
            for at in range(len(offsets)):
                to_pair(piece, at).wait_send()

    for k in range(1, layers):
        each_piece(k, finish)

    @pl.when(can_rise)
    def risen():
        relay(None, True).wait_send()

    @pl.when(can_fall)
    def fallen():
        relay(None, False).wait_send()

    for copy in back_layer + back_plane + keep:
        copy.wait()


def join_kernel(b_ref, a_ref, out_ref):
    block = b_ref.shape[-1]
    for p in range(b_ref.shape[1]):
        out_ref[:, p * block : (p + 1) * block] = b_ref[0, p] + a_ref[p, 0].T


def local(sizes, coeffs, hblocks, hcount, hcols):
    rows, cols, layers = sizes
    group = rows * cols
    row_count, col_count = coeffs.shape
    share, block, _ = hblocks.shape
    stored = share * layers
    blocks = row_count * group // block
    alpha_rows, beta_rows = col_count // group, row_count // layers
    per_layer, per_plane = blocks // layers, blocks // group
    beta_back = (layers, per_layer, beta_rows, block)
    alpha_back = (group, per_plane, alpha_rows, block)
    f32 = jnp.float32
    dma = pltpu.SemaphoreType.DMA

    row_end = jnp.cumsum(hcount)
    index = jnp.arange(stored, dtype=jnp.int32)
    owners = jnp.sum((row_end[None, :] <= index[:, None]).astype(jnp.int32), axis=1)
    keep = jnp.concatenate([jnp.zeros((1,), bool), owners[1:] == owners[:-1]])
    keep = (keep & (index % share != 0)).astype(f32)
    base = jnp.arange(layers, dtype=jnp.int32)[:, None] * share
    ends = jnp.minimum(row_end[None, :], base + share) - base
    starts = jnp.maximum((row_end - hcount)[None, :], base) - base
    found = (ends > starts).astype(f32).reshape(-1)
    last = jnp.clip(ends, 1, share).reshape(-1)

    padded = -(-share // 1024) * 1024
    names = jnp.pad(hcols, (0, padded - share)).reshape(-1, 128)
    flipped = coeffs.T.reshape(group, alpha_rows, row_count)
    chips = group // 2 if cols % 2 == 0 else group
    smem = pl.BlockSpec(memory_space=pltpu.SMEM)
    beta, alpha, _ = pl.pallas_call(
        functools.partial(sigma_kernel, sizes),
        out_shape=(
            jax.ShapeDtypeStruct(beta_back, f32),
            jax.ShapeDtypeStruct(alpha_back, f32),
            jax.ShapeDtypeStruct((layers, *names.shape), jnp.int32),
        ),
        in_specs=[ANY] * 4 + [smem] * 3,
        out_specs=(ANY,) * 3,
        scratch_shapes=[
            pltpu.VMEM((layers, beta_rows, col_count), f32),
            pltpu.VMEM((group, alpha_rows, row_count), f32),
            pltpu.VMEM((layers, share, block, block), f32),
            pltpu.VMEM((blocks, alpha_rows + beta_rows, 2 * block), jnp.bfloat16),
            pltpu.VMEM((share + 1, alpha_rows + beta_rows, block), f32),
            pltpu.VMEM(beta_back, f32),
            pltpu.VMEM(alpha_back, f32),
            pltpu.SMEM((layers, *names.shape), jnp.int32),
            dma((7,)),
        ]
        + ([dma((layers,))] * 2 + [dma((group,))] * 2) * 2
        + [dma((layers,))] * 5
        + [dma((layers, chips))] * 4,
        compiler_params=pltpu.CompilerParams(
            collective_id=0, has_side_effects=True, vmem_limit_bytes=56 * 2**20
        ),
        name="sigma",
    )(
        coeffs.reshape(layers, beta_rows, col_count),
        flipped,
        hblocks,
        names,
        keep,
        last,
        found,
    )
    if alpha_rows == block and beta_rows == block:
        return pl.pallas_call(
            join_kernel,
            out_shape=jax.ShapeDtypeStruct((row_count, col_count), f32),
            grid=(layers,),
            in_specs=[
                pl.BlockSpec((1, per_layer, block, block), lambda i: (i, 0, 0, 0)),
                pl.BlockSpec((group, 1, block, block), lambda i: (0, i, 0, 0)),
            ],
            out_specs=pl.BlockSpec((block, col_count), lambda i: (i, 0)),
            name="join",
        )(beta, alpha)
    beta = beta.transpose(0, 2, 1, 3).reshape(row_count, col_count)
    alpha = alpha.transpose(1, 3, 0, 2).reshape(row_count, col_count)
    return beta + alpha


def solution(mesh):
    sizes = tuple(mesh.shape[name] for name in ("row", "col", "layer"))
    in_specs = (P(("row", "col"), "layer"), P("layer", None, None), P(), P("layer"))
    out_specs = P(("row", "col"), "layer")
    return jax.shard_map(
        functools.partial(local, sizes),
        mesh=mesh,
        in_specs=in_specs,
        out_specs=out_specs,
        check_vma=False,
    )
```

```python
import functools

import jax
import jax.numpy as jnp
from jax import lax
from jax.experimental import pallas as pl
from jax.experimental.pallas import tpu as pltpu
from jax.sharding import PartitionSpec as P

MESH = pl.DeviceIdType.MESH
ANY = pl.BlockSpec(memory_space=pl.ANY)


def place():
    return lax.axis_index("row"), lax.axis_index("col"), lax.axis_index("layer")


def plane_peer(sizes, row, col, offset):
    rows, cols, _ = sizes
    down, right = offset // cols, offset % cols
    to = (lax.rem(row + down, rows), lax.rem(col + right, cols))
    source = lax.rem(row + rows - down, rows) * cols + lax.rem(col + cols - right, cols)
    return to, source


def greet(sizes):
    rows, cols, layers = sizes
    row, col, layer = place()
    barrier = pltpu.get_barrier_semaphore()
    for k in range(1, layers):
        to = (row, col, lax.rem(layer + k, layers))
        pl.semaphore_signal(barrier, inc=1, device_id=to, device_id_type=MESH)
    for offset in range(1, rows * cols):
        to, _ = plane_peer(sizes, row, col, offset)
        pl.semaphore_signal(barrier, inc=1, device_id=(*to, layer), device_id_type=MESH)
    pl.semaphore_wait(barrier, layers - 1 + rows * cols - 1)


def remote(src, dst, send_sem, recv_sem, to):
    return pltpu.make_async_remote_copy(
        src_ref=src,
        dst_ref=dst,
        send_sem=send_sem,
        recv_sem=recv_sem,
        device_id=to,
        device_id_type=MESH,
    )


def exchange(sizes, by_layer, by_plane, to_layer, to_plane, sems):
    rows, cols, layers = sizes
    row, col, layer = place()
    layer_send, layer_recv, plane_send, plane_recv = sems
    over_layer, over_plane = [], []
    for k in range(1, layers):
        other = lax.rem(layer + k, layers)
        over_layer.append(
            remote(
                by_layer(other),
                to_layer.at[layer],
                layer_send.at[k],
                layer_recv.at[k],
                (row, col, other),
            )
        )
    me = row * cols + col
    for offset in range(1, rows * cols):
        to, _ = plane_peer(sizes, row, col, offset)
        over_plane.append(
            remote(
                by_plane(to[0] * cols + to[1]),
                to_plane.at[me],
                plane_send.at[offset],
                plane_recv.at[offset],
                (*to, layer),
            )
        )
    return over_layer, over_plane


def halves(values):
    high = values.astype(jnp.bfloat16)
    low = (values - high.astype(jnp.float32)).astype(jnp.bfloat16)
    return high, low


def turn(held_ref, turned_ref):
    layers, width, block = turned_ref.shape
    for i in range(layers):
        for j in range(width // block):
            part = held_ref[i * block : (i + 1) * block, j * block : (j + 1) * block]
            turned_ref[i, j * block : (j + 1) * block, :] = part.T


def mark(count_ref, keep_ref, share):
    blocks = count_ref.shape[0]

    def body(n, carry):
        row, end = carry
        opens = n == end
        row = jnp.minimum(jnp.where(opens, row + 1, row), blocks - 1)
        end = jnp.where(opens, end + count_ref[row], end)
        keep_ref[n] = jnp.where(opens | (lax.rem(n, share) == 0), 0.0, 1.0)
        return row, end

    lax.fori_loop(0, keep_ref.shape[0], body, (jnp.int32(0), count_ref[0]))


def prepare(wide, ref, y_ref, block, beta):
    blocks = y_ref.shape[0]
    if wide:
        per = ref.shape[1] // block
        side = slice(block, 2 * block) if beta else slice(0, block)
        for j in range(blocks):
            high, low = halves(ref[j // per, (j % per) * block : (j % per + 1) * block, :])
            y_ref[j, :block, side] = high
            y_ref[j, block:, side] = low
        return
    per, count = ref.shape[2] // block, ref.shape[1]
    first = y_ref.shape[1] - count if beta else 0
    for j in range(blocks):
        high, low = halves(ref[j // per, :, (j % per) * block : (j % per + 1) * block])
        y_ref[j, first : first + count, :block] = high
        y_ref[j, first : first + count, block:] = low


def multiply(wide, piece, all_ref, names_ref, keep_ref, y_ref, sums_ref):
    _, share, block, _ = all_ref.shape
    group = 8 if share % 8 == 0 else 1

    def body(at, carry):
        results = []
        for i in range(group):
            n = at * group + i
            high, low = halves(all_ref[piece, n])
            four = jnp.concatenate(
                [jnp.concatenate([high, high], axis=1), jnp.concatenate([low, low], axis=1)], axis=0
            )
            picked = y_ref[names_ref[piece, 0, n]]
            if wide:
                both = jnp.dot(four, picked, preferred_element_type=jnp.float32)
                results.append(both[:block] + both[block:])
            else:
                both = lax.dot_general(
                    picked, four, (((1,), (1,)), ((), ())), preferred_element_type=jnp.float32
                )
                results.append(both[:, :block] + both[:, block:])
        running = sums_ref[at * group]
        for i in range(group):
            n = at * group + i
            running = results[i] + keep_ref[piece * share + n] * running
            sums_ref[n + 1] = running
        return carry

    lax.fori_loop(0, share // group, body, 0)


def gather(wide, piece, share, count_ref, sums_ref, a_ref, b_ref):
    alpha_rows, block = a_ref.shape[2:]
    per_a, per_b = a_ref.shape[1], b_ref.shape[1]
    base = piece * share

    def body(i, start):
        end = start + count_ref[i]
        low, high = jnp.maximum(start, base), jnp.minimum(end, base + share)
        found = jnp.where(high > low, 1.0, 0.0)
        part = found * sums_ref[jnp.clip(high - base, 1, share)]
        for_a = part[:, :block] if wide else part[:alpha_rows]
        for_b = part[:, block:] if wide else part[alpha_rows:]
        a_ref[lax.div(i, per_a), lax.rem(i, per_a)] += for_a
        b_ref[lax.div(i, per_b), lax.rem(i, per_b)] += for_b
        return end

    lax.fori_loop(0, count_ref.shape[0], body, jnp.int32(0))


def sigma_kernel(
    sizes,
    wide,
    c_ref,
    t_ref,
    h_ref,
    k_ref,
    count_ref,
    beta_ref,
    alpha_ref,
    cols_ref,
    z_ref,
    x_ref,
    all_ref,
    y_ref,
    sums_ref,
    b_ref,
    a_ref,
    names_ref,
    keep_ref,
    held_ref,
    turned_ref,
    own_sem,
    back_layer_send,
    back_layer_recv,
    back_plane_send,
    back_plane_recv,
    layer_send,
    layer_recv,
    plane_send,
    plane_recv,
    cols_send,
    cols_recv,
    rise_send,
    fall_send,
    relay_recv,
    chip_send,
    chip_recv,
    pair_send,
    pair_recv,
):
    rows, cols, layers = sizes
    row, col, layer = place()
    me = row * cols + col
    step = 2 if cols % 2 == 0 else 1
    offsets = [d * cols + e for d in range(rows) for e in range(0, cols, step)]
    share, block, _ = h_ref.shape
    size = share // (rows * cols)
    half = size // 2
    square = rows == 2 and cols == 4 and half > 0

    def for_layer(i):
        return turned_ref.at[i] if wide else c_ref.at[i]

    def for_plane(i):
        if wide:
            return t_ref.at[:, pl.ds(pl.multiple_of(i * block, block), block)]
        return t_ref.at[i]

    def piece_at(piece, source):
        return all_ref.at[piece, pl.ds(pl.multiple_of(source * size, size), size)]

    greet(sizes)

    def relay(piece, up):
        mine = h_ref.at[pl.ds(pl.multiple_of(me * size, size), size)]
        src = mine if piece is None else piece_at(piece, me)
        piece = layer if piece is None else piece
        sem = rise_send if up else fall_send
        to = (row, col, layer + 1 if up else layer - 1)
        return remote(src, piece_at(piece, me), sem.at[piece], relay_recv.at[piece], to)

    def to_chip(piece, at):
        to, _ = plane_peer(sizes, row, col, offsets[at])
        return remote(
            piece_at(piece, me),
            piece_at(piece, me),
            chip_send.at[piece, at],
            chip_recv.at[piece, at],
            (*to, layer),
        )

    def to_corner(piece, part):
        _, source = plane_peer(sizes, row, col, offsets[1 + part])
        to, _ = plane_peer(sizes, row, col, offsets[2 - part])
        first = pl.multiple_of(source * size + part * half, half)
        part_ref = all_ref.at[piece, pl.ds(first, half)]
        at = 0 if part == 0 else 3
        sems = chip_send.at[piece, at], chip_recv.at[piece, at]
        return remote(part_ref, part_ref, *sems, (*to, layer))

    def to_pair(piece, at):
        _, source = plane_peer(sizes, row, col, offsets[at])
        twin = (row, col + 1 - 2 * lax.rem(col, 2), layer)
        return remote(
            piece_at(piece, source),
            piece_at(piece, source),
            pair_send.at[piece, at],
            pair_recv.at[piece, at],
            twin,
        )

    chips = [1, 2] if square else list(range(1, len(offsets)))

    def each_piece(k, act):
        @pl.when(layer >= k)
        def below():
            act(layer - k, True)

        @pl.when(layer + k < layers)
        def above():
            act(layer + k, False)

    can_rise, can_fall = layer + 1 < layers, layer > 0

    @pl.when(can_rise)
    def rise():
        relay(None, True).start()

    @pl.when(can_fall)
    def fall():
        relay(None, False).start()

    over_layer, over_plane = exchange(
        sizes, for_layer, for_plane, z_ref, x_ref, (layer_send, layer_recv, plane_send, plane_recv)
    )
    names = []
    for k in range(1, layers):
        to = (row, col, lax.rem(layer + k, layers))
        names.append(remote(k_ref, cols_ref.at[layer], cols_send.at[k], cols_recv.at[k], to))
    own = [
        pltpu.make_async_copy(for_layer(layer), z_ref.at[layer], own_sem.at[0]),
        pltpu.make_async_copy(for_plane(me), x_ref.at[me], own_sem.at[1]),
        pltpu.make_async_copy(k_ref, cols_ref.at[layer], own_sem.at[2]),
        pltpu.make_async_copy(h_ref, all_ref.at[layer], own_sem.at[3]),
    ]
    if wide:
        held = pltpu.make_async_copy(c_ref, held_ref, own_sem.at[7])
        held.start()
    for copy in names + over_plane + own[1:]:
        copy.start()
    if wide:
        held.wait()
        turn(held_ref, turned_ref)
    own[0].start()
    mark(count_ref, keep_ref, share)

    def arrive(piece, upward):
        relay(piece, upward).wait_recv()

        @pl.when(can_rise if upward else can_fall)
        def onward():
            relay(piece, upward).start()

        for at in chips:
            to_chip(piece, at).start()
        if step == 2:
            to_pair(piece, 0).start()

    def pass_on(piece, upward):
        for at in chips:
            to_chip(piece, at).wait_recv()
            if square:
                to_corner(piece, at - 1).start()
            if step == 2:
                to_pair(piece, at).start()

    def pass_corner(piece, upward):
        if square:
            to_corner(piece, 0).wait_recv()
            to_corner(piece, 1).wait_recv()
            to_pair(piece, 3).start()

    early = min(2, layers - 1)
    for k in range(1, layers):
        each_piece(k, arrive)
        if k == early:
            for copy in over_layer:
                copy.start()
        if k > 1 and k < layers - 1:
            each_piece(k - 1, pass_on)
    if layers > 2:
        each_piece(layers - 2, pass_on)
    for k in range(1, layers - 2):
        each_piece(k, pass_corner)
    if layers > 1:
        each_piece(layers - 1, pass_on)
    if layers > 2:
        each_piece(layers - 2, pass_corner)

    for copy in names + over_plane + own[:3]:
        copy.wait()
    prepare(wide, x_ref, y_ref, block, False)
    a_ref[...] = jnp.zeros_like(a_ref)
    b_ref[...] = jnp.zeros_like(b_ref)
    sums_ref[0] = jnp.zeros_like(sums_ref[0])
    to_scalars = pltpu.make_async_copy(cols_ref, names_ref, own_sem.at[4])
    to_scalars.start()
    for copy in over_layer:
        copy.wait()
    prepare(wide, z_ref, y_ref, block, True)
    to_scalars.wait()
    own[3].wait()

    sign = 1 - 2 * lax.div(2 * layer, layers)

    def treat(t, carry):
        piece = lax.rem(layer + layers + t * sign, layers)

        if step == 2:

            @pl.when(t > 0)
            def complete():
                for at in range(len(offsets)):
                    to_pair(piece, at).wait_recv()

        multiply(wide, piece, all_ref, names_ref, keep_ref, y_ref, sums_ref)
        gather(wide, piece, share, count_ref, sums_ref, a_ref, b_ref)

        @pl.when(t == 0)
        def corners():
            if layers > 1:
                each_piece(layers - 1, pass_corner)

        return carry

    lax.fori_loop(0, layers, treat, 0)

    sems = (back_layer_send, back_layer_recv, back_plane_send, back_plane_recv)
    back_layer, back_plane = exchange(
        sizes, lambda i: b_ref.at[i], lambda i: a_ref.at[i], beta_ref, alpha_ref, sems
    )
    keep = [
        pltpu.make_async_copy(b_ref.at[layer], beta_ref.at[layer], own_sem.at[5]),
        pltpu.make_async_copy(a_ref.at[me], alpha_ref.at[me], own_sem.at[6]),
    ]
    for copy in back_layer + back_plane + keep:
        copy.start()

    def finish(piece, upward):
        @pl.when(can_rise if upward else can_fall)
        def sent():
            relay(piece, upward).wait_send()

        for at in chips:
            to_chip(piece, at).wait_send()
        if square:
            to_corner(piece, 0).wait_send()
            to_corner(piece, 1).wait_send()
        if step == 2:
            for at in range(len(offsets)):
                to_pair(piece, at).wait_send()

    for k in range(1, layers):
        each_piece(k, finish)

    @pl.when(can_rise)
    def risen():
        relay(None, True).wait_send()

    @pl.when(can_fall)
    def fallen():
        relay(None, False).wait_send()

    for copy in back_layer + back_plane + keep:
        copy.wait()


def join_kernel(b_ref, a_ref, out_ref):
    block = b_ref.shape[-1]
    for p in range(b_ref.shape[1]):
        out_ref[:, p * block : (p + 1) * block] = b_ref[0, p].T + a_ref[p, 0]


def local(sizes, coeffs, hblocks, hcount, hcols):
    rows, cols, layers = sizes
    group = rows * cols
    row_count, col_count = coeffs.shape
    share, block, _ = hblocks.shape
    stored = share * layers
    blocks = row_count * group // block
    alpha_rows, beta_rows = col_count // group, row_count // layers
    per_layer, per_plane = blocks // layers, blocks // group
    beta_back = (layers, per_layer, beta_rows, block)
    alpha_back = (group, per_plane, alpha_rows, block)
    f32 = jnp.float32
    dma = pltpu.SemaphoreType.DMA

    wide = alpha_rows == block and beta_rows == block
    names = hcols.reshape(1, share)
    if wide:
        for_layer, for_plane = coeffs, coeffs
        z_shape, x_shape = (layers, col_count, block), (group, row_count, block)
        y_shape, sum_shape = (blocks, 2 * block, 2 * block), (share + 1, block, 2 * block)
        held, turned = coeffs.shape, z_shape
    else:
        for_layer = coeffs.reshape(layers, beta_rows, col_count)
        for_plane = coeffs.T.reshape(group, alpha_rows, row_count)
        z_shape, x_shape = for_layer.shape, for_plane.shape
        both = alpha_rows + beta_rows
        y_shape, sum_shape = (blocks, both, 2 * block), (share + 1, both, block)
        held = turned = (8, 128)
    chips = group // 2 if cols % 2 == 0 else group
    smem = pl.BlockSpec(memory_space=pltpu.SMEM)
    beta, alpha, _ = pl.pallas_call(
        functools.partial(sigma_kernel, sizes, wide),
        out_shape=(
            jax.ShapeDtypeStruct(beta_back, f32),
            jax.ShapeDtypeStruct(alpha_back, f32),
            jax.ShapeDtypeStruct((layers, *names.shape), jnp.int32),
        ),
        in_specs=[ANY] * 4 + [smem],
        out_specs=(ANY,) * 3,
        scratch_shapes=[
            pltpu.VMEM(z_shape, f32),
            pltpu.VMEM(x_shape, f32),
            pltpu.VMEM((layers, share, block, block), f32),
            pltpu.VMEM(y_shape, jnp.bfloat16),
            pltpu.VMEM(sum_shape, f32),
            pltpu.VMEM(beta_back, f32),
            pltpu.VMEM(alpha_back, f32),
            pltpu.SMEM((layers, *names.shape), jnp.int32),
            pltpu.SMEM((stored,), f32),
            pltpu.VMEM(held, f32),
            pltpu.VMEM(turned, f32),
            dma((8,)),
        ]
        + ([dma((layers,))] * 2 + [dma((group,))] * 2) * 2
        + [dma((layers,))] * 5
        + [dma((layers, chips))] * 4,
        compiler_params=pltpu.CompilerParams(
            collective_id=0, has_side_effects=True, vmem_limit_bytes=56 * 2**20
        ),
        name="sigma",
    )(
        for_layer,
        for_plane,
        hblocks,
        names,
        hcount,
    )
    if wide:
        return pl.pallas_call(
            join_kernel,
            out_shape=jax.ShapeDtypeStruct((row_count, col_count), f32),
            grid=(layers,),
            in_specs=[
                pl.BlockSpec((1, per_layer, block, block), lambda i: (i, 0, 0, 0)),
                pl.BlockSpec((group, 1, block, block), lambda i: (0, i, 0, 0)),
            ],
            out_specs=pl.BlockSpec((block, col_count), lambda i: (i, 0)),
            name="join",
        )(beta, alpha)
    beta = beta.transpose(0, 2, 1, 3).reshape(row_count, col_count)
    alpha = alpha.transpose(1, 3, 0, 2).reshape(row_count, col_count)
    return beta + alpha


def solution(mesh):
    sizes = tuple(mesh.shape[name] for name in ("row", "col", "layer"))
    in_specs = (P(("row", "col"), "layer"), P("layer", None, None), P(), P("layer"))
    out_specs = P(("row", "col"), "layer")
    return jax.shard_map(
        functools.partial(local, sizes),
        mesh=mesh,
        in_specs=in_specs,
        out_specs=out_specs,
        check_vma=False,
    )
```

```python
import functools

import jax
import jax.numpy as jnp
from jax import lax
from jax.experimental import pallas as pl
from jax.experimental.pallas import tpu as pltpu
from jax.sharding import PartitionSpec as P

MESH = pl.DeviceIdType.MESH
ANY = pl.BlockSpec(memory_space=pl.ANY)


def place():
    return lax.axis_index("row"), lax.axis_index("col"), lax.axis_index("layer")


def plane_peer(sizes, row, col, offset):
    rows, cols, _ = sizes
    down, right = offset // cols, offset % cols
    to = (lax.rem(row + down, rows), lax.rem(col + right, cols))
    source = lax.rem(row + rows - down, rows) * cols + lax.rem(col + cols - right, cols)
    return to, source


def greet(sizes):
    rows, cols, layers = sizes
    row, col, layer = place()
    barrier = pltpu.get_barrier_semaphore()
    for k in range(1, layers):
        to = (row, col, lax.rem(layer + k, layers))
        pl.semaphore_signal(barrier, inc=1, device_id=to, device_id_type=MESH)
    for offset in range(1, rows * cols):
        to, _ = plane_peer(sizes, row, col, offset)
        pl.semaphore_signal(barrier, inc=1, device_id=(*to, layer), device_id_type=MESH)
    pl.semaphore_wait(barrier, layers - 1 + rows * cols - 1)


def remote(src, dst, send_sem, recv_sem, to):
    return pltpu.make_async_remote_copy(
        src_ref=src,
        dst_ref=dst,
        send_sem=send_sem,
        recv_sem=recv_sem,
        device_id=to,
        device_id_type=MESH,
    )


def exchange(sizes, by_layer, by_plane, to_layer, to_plane, sems):
    rows, cols, layers = sizes
    row, col, layer = place()
    layer_send, layer_recv, plane_send, plane_recv = sems
    over_layer, over_plane = [], []
    for k in range(1, layers):
        other = lax.rem(layer + k, layers)
        over_layer.append(
            remote(
                by_layer(other),
                to_layer.at[layer],
                layer_send.at[k],
                layer_recv.at[k],
                (row, col, other),
            )
        )
    me = row * cols + col
    for offset in range(1, rows * cols):
        to, _ = plane_peer(sizes, row, col, offset)
        over_plane.append(
            remote(
                by_plane(to[0] * cols + to[1]),
                to_plane.at[me],
                plane_send.at[offset],
                plane_recv.at[offset],
                (*to, layer),
            )
        )
    return over_layer, over_plane


def halves(values):
    high = values.astype(jnp.bfloat16)
    low = (values - high.astype(jnp.float32)).astype(jnp.bfloat16)
    return high, low


def turn(held_ref, turned_ref):
    layers, width, block = turned_ref.shape
    for i in range(layers):
        for j in range(width // block):
            part = held_ref[i * block : (i + 1) * block, j * block : (j + 1) * block]
            turned_ref[i, j * block : (j + 1) * block, :] = part.T


def mark(count_ref, keep_ref, share):
    blocks = count_ref.shape[0]

    def body(n, carry):
        row, end = carry
        opens = n == end
        row = jnp.minimum(jnp.where(opens, row + 1, row), blocks - 1)
        end = jnp.where(opens, end + count_ref[row], end)
        keep_ref[n] = jnp.where(opens | (lax.rem(n, share) == 0), 0.0, 1.0)
        return row, end

    lax.fori_loop(0, keep_ref.shape[0], body, (jnp.int32(0), count_ref[0]))


def prepare(wide, ref, i, y_ref, block, beta):
    if wide:
        per = ref.shape[1] // block
        side = slice(block, 2 * block) if beta else slice(0, block)
        for j in range(per):
            high, low = halves(ref[i, j * block : (j + 1) * block, :])
            y_ref[i * per + j, :block, side] = high
            y_ref[i * per + j, block:, side] = low
        return
    per, count = ref.shape[2] // block, ref.shape[1]
    first = y_ref.shape[1] - count if beta else 0
    for j in range(per):
        high, low = halves(ref[i, :, j * block : (j + 1) * block])
        y_ref[i * per + j, first : first + count, :block] = high
        y_ref[i * per + j, first : first + count, block:] = low


def multiply(wide, piece, all_ref, names_ref, keep_ref, y_ref, sums_ref):
    _, share, block, _ = all_ref.shape
    group = 8 if share % 8 == 0 else 1

    def body(at, carry):
        running = sums_ref[at * group]
        for i in range(group):
            n = at * group + i
            high, low = halves(all_ref[piece, n])
            four = jnp.concatenate(
                [jnp.concatenate([high, high], axis=1), jnp.concatenate([low, low], axis=1)], axis=0
            )
            picked = y_ref[names_ref[piece, 0, n]]
            if wide:
                both = jnp.dot(four, picked, preferred_element_type=jnp.float32)
                result = both[:block] + both[block:]
            else:
                both = lax.dot_general(
                    picked, four, (((1,), (1,)), ((), ())), preferred_element_type=jnp.float32
                )
                result = both[:, :block] + both[:, block:]
            running = result + keep_ref[piece * share + n] * running
            sums_ref[n + 1] = running
        return carry

    lax.fori_loop(0, share // group, body, 0)


def gather(wide, piece, share, count_ref, sums_ref, a_ref, b_ref):
    alpha_rows, block = a_ref.shape[2:]
    per_a, per_b = a_ref.shape[1], b_ref.shape[1]
    base = piece * share

    def body(i, start):
        end = start + count_ref[i]
        low, high = jnp.maximum(start, base), jnp.minimum(end, base + share)
        found = jnp.where(high > low, 1.0, 0.0)
        part = found * sums_ref[jnp.clip(high - base, 1, share)]
        for_a = part[:, :block] if wide else part[:alpha_rows]
        for_b = part[:, block:] if wide else part[alpha_rows:]
        a_ref[lax.div(i, per_a), lax.rem(i, per_a)] += for_a
        b_ref[lax.div(i, per_b), lax.rem(i, per_b)] += for_b
        return end

    lax.fori_loop(0, count_ref.shape[0], body, jnp.int32(0))


def sigma_kernel(
    sizes,
    wide,
    c_ref,
    t_ref,
    h_ref,
    k_ref,
    count_ref,
    beta_ref,
    alpha_ref,
    cols_ref,
    z_ref,
    x_ref,
    all_ref,
    y_ref,
    sums_ref,
    b_ref,
    a_ref,
    names_ref,
    keep_ref,
    held_ref,
    turned_ref,
    own_sem,
    back_layer_send,
    back_layer_recv,
    back_plane_send,
    back_plane_recv,
    layer_send,
    layer_recv,
    plane_send,
    plane_recv,
    cols_send,
    cols_recv,
    rise_send,
    fall_send,
    relay_recv,
    chip_send,
    chip_recv,
    pair_send,
    pair_recv,
    out_ref=None,
):
    rows, cols, layers = sizes
    row, col, layer = place()
    me = row * cols + col
    step = 2 if cols % 2 == 0 else 1
    offsets = [d * cols + e for d in range(rows) for e in range(0, cols, step)]
    share, block, _ = h_ref.shape
    size = share // (rows * cols)
    half = size // 2
    square = rows == 2 and cols == 4 and half > 0

    def for_layer(i):
        return turned_ref.at[i] if wide else c_ref.at[i]

    def for_plane(i):
        if wide:
            return t_ref.at[:, pl.ds(pl.multiple_of(i * block, block), block)]
        return t_ref.at[i]

    def piece_at(piece, source):
        return all_ref.at[piece, pl.ds(pl.multiple_of(source * size, size), size)]

    greet(sizes)

    def relay(piece, up):
        mine = h_ref.at[pl.ds(pl.multiple_of(me * size, size), size)]
        src = mine if piece is None else piece_at(piece, me)
        piece = layer if piece is None else piece
        sem = rise_send if up else fall_send
        to = (row, col, layer + 1 if up else layer - 1)
        return remote(src, piece_at(piece, me), sem.at[piece], relay_recv.at[piece], to)

    def to_chip(piece, at):
        to, _ = plane_peer(sizes, row, col, offsets[at])
        return remote(
            piece_at(piece, me),
            piece_at(piece, me),
            chip_send.at[piece, at],
            chip_recv.at[piece, at],
            (*to, layer),
        )

    def to_corner(piece, part):
        _, source = plane_peer(sizes, row, col, offsets[1 + part])
        to, _ = plane_peer(sizes, row, col, offsets[2 - part])
        first = pl.multiple_of(source * size + part * half, half)
        part_ref = all_ref.at[piece, pl.ds(first, half)]
        at = 0 if part == 0 else 3
        sems = chip_send.at[piece, at], chip_recv.at[piece, at]
        return remote(part_ref, part_ref, *sems, (*to, layer))

    def to_pair(piece, at):
        _, source = plane_peer(sizes, row, col, offsets[at])
        twin = (row, col + 1 - 2 * lax.rem(col, 2), layer)
        return remote(
            piece_at(piece, source),
            piece_at(piece, source),
            pair_send.at[piece, at],
            pair_recv.at[piece, at],
            twin,
        )

    chips = [1, 2] if square else list(range(1, len(offsets)))

    def each_piece(k, act):
        @pl.when(layer >= k)
        def below():
            act(layer - k, True)

        @pl.when(layer + k < layers)
        def above():
            act(layer + k, False)

    can_rise, can_fall = layer + 1 < layers, layer > 0

    @pl.when(can_rise)
    def rise():
        relay(None, True).start()

    @pl.when(can_fall)
    def fall():
        relay(None, False).start()

    over_layer, over_plane = exchange(
        sizes, for_layer, for_plane, z_ref, x_ref, (layer_send, layer_recv, plane_send, plane_recv)
    )
    names = []
    for k in range(1, layers):
        to = (row, col, lax.rem(layer + k, layers))
        names.append(remote(k_ref, cols_ref.at[layer], cols_send.at[k], cols_recv.at[k], to))
    own = [
        pltpu.make_async_copy(for_layer(layer), z_ref.at[layer], own_sem.at[0]),
        pltpu.make_async_copy(for_plane(me), x_ref.at[me], own_sem.at[1]),
        pltpu.make_async_copy(k_ref, cols_ref.at[layer], own_sem.at[2]),
        pltpu.make_async_copy(h_ref, all_ref.at[layer], own_sem.at[3]),
    ]
    if wide:
        held = pltpu.make_async_copy(c_ref, held_ref, own_sem.at[7])
        held.start()
    for copy in names + over_plane + own[1:]:
        copy.start()
    if wide:
        held.wait()
        turn(held_ref, turned_ref)
    own[0].start()
    mark(count_ref, keep_ref, share)

    def arrive(piece, upward):
        relay(piece, upward).wait_recv()

        @pl.when(can_rise if upward else can_fall)
        def onward():
            relay(piece, upward).start()

        for at in chips:
            to_chip(piece, at).start()
        if step == 2:
            to_pair(piece, 0).start()

    def pass_on(piece, upward):
        for at in chips:
            to_chip(piece, at).wait_recv()
            if square:
                to_corner(piece, at - 1).start()
            if step == 2:
                to_pair(piece, at).start()

    def pass_corner(piece, upward):
        if square:
            to_corner(piece, 0).wait_recv()
            to_corner(piece, 1).wait_recv()
            to_pair(piece, 3).start()

    early = min(2, layers - 1)
    for k in range(1, layers):
        each_piece(k, arrive)
        if k == early:
            for copy in over_layer:
                copy.start()
        if k > 1 and k < layers - 1:
            each_piece(k - 1, pass_on)
    if layers > 2:
        each_piece(layers - 2, pass_on)
    for k in range(1, layers - 2):
        each_piece(k, pass_corner)
    if layers > 1:
        each_piece(layers - 1, pass_on)
    if layers > 2:
        each_piece(layers - 2, pass_corner)

    for copy in names + over_plane + own[:3]:
        copy.wait()
    for i in range(rows * cols):
        prepare(wide, x_ref, i, y_ref, block, False)
    prepare(wide, z_ref, layer, y_ref, block, True)
    a_ref[...] = jnp.zeros_like(a_ref)
    b_ref[...] = jnp.zeros_like(b_ref)
    sums_ref[0] = jnp.zeros_like(sums_ref[0])
    to_scalars = pltpu.make_async_copy(cols_ref, names_ref, own_sem.at[4])
    to_scalars.start()
    for k, copy in enumerate(over_layer, 1):
        copy.wait()
        prepare(wide, z_ref, lax.rem(layer + layers - k, layers), y_ref, block, True)
    to_scalars.wait()
    own[3].wait()

    sign = 1 - 2 * lax.div(2 * layer, layers)

    def treat(t, carry):
        piece = lax.rem(layer + layers + t * sign, layers)

        if step == 2:

            @pl.when(t > 0)
            def complete():
                for at in range(len(offsets)):
                    to_pair(piece, at).wait_recv()

        multiply(wide, piece, all_ref, names_ref, keep_ref, y_ref, sums_ref)
        gather(wide, piece, share, count_ref, sums_ref, a_ref, b_ref)

        @pl.when(t == 0)
        def corners():
            if layers > 1:
                each_piece(layers - 1, pass_corner)

        return carry

    lax.fori_loop(0, layers, treat, 0)

    sems = (back_layer_send, back_layer_recv, back_plane_send, back_plane_recv)
    back_layer, back_plane = exchange(
        sizes, lambda i: b_ref.at[i], lambda i: a_ref.at[i], beta_ref, alpha_ref, sems
    )
    keep = [
        pltpu.make_async_copy(b_ref.at[layer], beta_ref.at[layer], own_sem.at[5]),
        pltpu.make_async_copy(a_ref.at[me], alpha_ref.at[me], own_sem.at[6]),
    ]
    for copy in back_layer + back_plane + keep:
        copy.start()

    def finish(piece, upward):
        @pl.when(can_rise if upward else can_fall)
        def sent():
            relay(piece, upward).wait_send()

        for at in chips:
            to_chip(piece, at).wait_send()
        if square:
            to_corner(piece, 0).wait_send()
            to_corner(piece, 1).wait_send()
        if step == 2:
            for at in range(len(offsets)):
                to_pair(piece, at).wait_send()

    for k in range(1, layers):
        each_piece(k, finish)

    @pl.when(can_rise)
    def risen():
        relay(None, True).wait_send()

    @pl.when(can_fall)
    def fallen():
        relay(None, False).wait_send()

    for copy in back_plane + keep:
        copy.wait()

    def join(i):
        for p in range(rows * cols):
            at = pl.ds(pl.multiple_of(i * block, block), block)
            out_ref[at, p * block : (p + 1) * block] = beta_ref[i, p].T + alpha_ref[p, i]

    if wide:
        join(layer)
    for k, copy in enumerate(back_layer, 1):
        copy.wait()
        if wide:
            join(lax.rem(layer + layers - k, layers))


def wide_kernel(sizes, c, t, h, k, count, out_ref, columns, beta, alpha, *scratch):
    sigma_kernel(sizes, True, c, t, h, k, count, beta, alpha, columns, *scratch, out_ref=out_ref)


def local(sizes, coeffs, hblocks, hcount, hcols):
    rows, cols, layers = sizes
    group = rows * cols
    row_count, col_count = coeffs.shape
    share, block, _ = hblocks.shape
    stored = share * layers
    blocks = row_count * group // block
    alpha_rows, beta_rows = col_count // group, row_count // layers
    per_layer, per_plane = blocks // layers, blocks // group
    beta_back = (layers, per_layer, beta_rows, block)
    alpha_back = (group, per_plane, alpha_rows, block)
    f32 = jnp.float32
    dma = pltpu.SemaphoreType.DMA

    wide = alpha_rows == block and beta_rows == block
    names = hcols.reshape(1, share)
    if wide:
        for_layer, for_plane = coeffs, coeffs
        z_shape, x_shape = (layers, col_count, block), (group, row_count, block)
        y_shape, sum_shape = (blocks, 2 * block, 2 * block), (share + 1, block, 2 * block)
        held, turned = coeffs.shape, z_shape
    else:
        for_layer = coeffs.reshape(layers, beta_rows, col_count)
        for_plane = coeffs.T.reshape(group, alpha_rows, row_count)
        z_shape, x_shape = for_layer.shape, for_plane.shape
        both = alpha_rows + beta_rows
        y_shape, sum_shape = (blocks, both, 2 * block), (share + 1, both, block)
        held = turned = (8, 128)
    chips = group // 2 if cols % 2 == 0 else group
    smem = pl.BlockSpec(memory_space=pltpu.SMEM)
    gathered = jax.ShapeDtypeStruct((layers, *names.shape), jnp.int32)
    if wide:
        kernel = functools.partial(wide_kernel, sizes)
        out_shape = (jax.ShapeDtypeStruct((row_count, col_count), f32), gathered)
        out_specs = (pl.BlockSpec(memory_space=pltpu.VMEM), ANY)
        landing = [pltpu.VMEM(beta_back, f32), pltpu.VMEM(alpha_back, f32)]
    else:
        kernel = functools.partial(sigma_kernel, sizes, False)
        out_shape = (
            jax.ShapeDtypeStruct(beta_back, f32),
            jax.ShapeDtypeStruct(alpha_back, f32),
            gathered,
        )
        out_specs = (ANY,) * 3
        landing = []
    results = pl.pallas_call(
        kernel,
        out_shape=out_shape,
        in_specs=[ANY] * 4 + [smem],
        out_specs=out_specs,
        scratch_shapes=landing
        + [
            pltpu.VMEM(z_shape, f32),
            pltpu.VMEM(x_shape, f32),
            pltpu.VMEM((layers, share, block, block), f32),
            pltpu.VMEM(y_shape, jnp.bfloat16),
            pltpu.VMEM(sum_shape, f32),
            pltpu.VMEM(beta_back, f32),
            pltpu.VMEM(alpha_back, f32),
            pltpu.SMEM((layers, *names.shape), jnp.int32),
            pltpu.SMEM((stored,), f32),
            pltpu.VMEM(held, f32),
            pltpu.VMEM(turned, f32),
            dma((8,)),
        ]
        + ([dma((layers,))] * 2 + [dma((group,))] * 2) * 2
        + [dma((layers,))] * 5
        + [dma((layers, chips))] * 4,
        compiler_params=pltpu.CompilerParams(
            collective_id=0, has_side_effects=True, vmem_limit_bytes=56 * 2**20
        ),
        name="sigma",
    )(
        for_layer,
        for_plane,
        hblocks,
        names,
        hcount,
    )
    if wide:
        return results[0]
    beta, alpha, _ = results
    beta = beta.transpose(0, 2, 1, 3).reshape(row_count, col_count)
    alpha = alpha.transpose(1, 3, 0, 2).reshape(row_count, col_count)
    return beta + alpha


def solution(mesh):
    sizes = tuple(mesh.shape[name] for name in ("row", "col", "layer"))
    in_specs = (P(("row", "col"), "layer"), P("layer", None, None), P(), P("layer"))
    out_specs = P(("row", "col"), "layer")
    return jax.shard_map(
        functools.partial(local, sizes),
        mesh=mesh,
        in_specs=in_specs,
        out_specs=out_specs,
        check_vma=False,
    )
```

```python
import functools

import jax
import jax.numpy as jnp
from jax import lax
from jax.experimental import pallas as pl
from jax.experimental.pallas import tpu as pltpu
from jax.sharding import PartitionSpec as P

MESH = pl.DeviceIdType.MESH
ANY = pl.BlockSpec(memory_space=pl.ANY)


def place():
    return lax.axis_index("row"), lax.axis_index("col"), lax.axis_index("layer")


def plane_peer(sizes, row, col, offset):
    rows, cols, _ = sizes
    down, right = offset // cols, offset % cols
    to = (lax.rem(row + down, rows), lax.rem(col + right, cols))
    source = lax.rem(row + rows - down, rows) * cols + lax.rem(col + cols - right, cols)
    return to, source


def greet(sizes):
    rows, cols, layers = sizes
    row, col, layer = place()
    barrier = pltpu.get_barrier_semaphore()
    for k in range(1, layers):
        to = (row, col, lax.rem(layer + k, layers))
        pl.semaphore_signal(barrier, inc=1, device_id=to, device_id_type=MESH)
    for offset in range(1, rows * cols):
        to, _ = plane_peer(sizes, row, col, offset)
        pl.semaphore_signal(barrier, inc=1, device_id=(*to, layer), device_id_type=MESH)
    pl.semaphore_wait(barrier, layers - 1 + rows * cols - 1)


def remote(src, dst, send_sem, recv_sem, to):
    return pltpu.make_async_remote_copy(
        src_ref=src,
        dst_ref=dst,
        send_sem=send_sem,
        recv_sem=recv_sem,
        device_id=to,
        device_id_type=MESH,
    )


def exchange(sizes, by_layer, by_plane, to_layer, to_plane, sems):
    rows, cols, layers = sizes
    row, col, layer = place()
    layer_send, layer_recv, plane_send, plane_recv = sems
    over_layer, over_plane = [], []
    for k in range(1, layers):
        other = lax.rem(layer + k, layers)
        over_layer.append(
            remote(
                by_layer(other),
                to_layer.at[layer],
                layer_send.at[k],
                layer_recv.at[k],
                (row, col, other),
            )
        )
    me = row * cols + col
    for offset in range(1, rows * cols):
        to, _ = plane_peer(sizes, row, col, offset)
        over_plane.append(
            remote(
                by_plane(to[0] * cols + to[1]),
                to_plane.at[me],
                plane_send.at[offset],
                plane_recv.at[offset],
                (*to, layer),
            )
        )
    return over_layer, over_plane


def halves(values):
    high = values.astype(jnp.bfloat16)
    low = (values - high.astype(jnp.float32)).astype(jnp.bfloat16)
    return high, low


def turn(held_ref, turned_ref):
    layers, width, block = turned_ref.shape
    for i in range(layers):
        for j in range(width // block):
            part = held_ref[i * block : (i + 1) * block, j * block : (j + 1) * block]
            turned_ref[i, j * block : (j + 1) * block, :] = part.T


def mark(count_ref, keep_ref, share):
    blocks = count_ref.shape[0]

    def body(n, carry):
        row, end = carry
        opens = n == end
        row = jnp.minimum(jnp.where(opens, row + 1, row), blocks - 1)
        end = jnp.where(opens, end + count_ref[row], end)
        keep_ref[n] = jnp.where(opens | (lax.rem(n, share) == 0), 0.0, 1.0)
        return row, end

    lax.fori_loop(0, keep_ref.shape[0], body, (jnp.int32(0), count_ref[0]))


def prepare(wide, ref, i, y_ref, block, beta):
    if wide:
        per = ref.shape[1] // block
        side = slice(block, 2 * block) if beta else slice(0, block)
        for j in range(per):
            high, low = halves(ref[i, j * block : (j + 1) * block, :])
            y_ref[i * per + j, :block, side] = high
            y_ref[i * per + j, block:, side] = low
        return
    per, count = ref.shape[2] // block, ref.shape[1]
    first = y_ref.shape[1] - count if beta else 0
    for j in range(per):
        high, low = halves(ref[i, :, j * block : (j + 1) * block])
        y_ref[i * per + j, first : first + count, :block] = high
        y_ref[i * per + j, first : first + count, block:] = low


def multiply(wide, piece, all_ref, names_ref, keep_ref, y_ref, sums_ref):
    _, share, block, _ = all_ref.shape
    group = 8 if share % 8 == 0 else 1

    def body(at, carry):
        running = sums_ref[at * group]
        for i in range(group):
            n = at * group + i
            high, low = halves(all_ref[piece, n])
            four = jnp.concatenate(
                [jnp.concatenate([high, high], axis=1), jnp.concatenate([low, low], axis=1)], axis=0
            )
            picked = y_ref[names_ref[piece, 0, n]]
            if wide:
                both = jnp.dot(four, picked, preferred_element_type=jnp.float32)
                result = both[:block] + both[block:]
            else:
                both = lax.dot_general(
                    picked, four, (((1,), (1,)), ((), ())), preferred_element_type=jnp.float32
                )
                result = both[:, :block] + both[:, block:]
            running = result + keep_ref[piece * share + n] * running
            sums_ref[n + 1] = running
        return carry

    lax.fori_loop(0, share // group, body, 0)


def gather(wide, piece, share, count_ref, sums_ref, a_ref, b_ref):
    alpha_rows, block = a_ref.shape[2:]
    per_a, per_b = a_ref.shape[1], b_ref.shape[1]
    base = piece * share

    def body(i, start):
        end = start + count_ref[i]
        low, high = jnp.maximum(start, base), jnp.minimum(end, base + share)
        found = jnp.where(high > low, 1.0, 0.0)
        part = found * sums_ref[jnp.clip(high - base, 1, share)]
        for_a = part[:, :block] if wide else part[:alpha_rows]
        for_b = part[:, block:] if wide else part[alpha_rows:]
        a_ref[lax.div(i, per_a), lax.rem(i, per_a)] += for_a
        b_ref[lax.div(i, per_b), lax.rem(i, per_b)] += for_b
        return end

    lax.fori_loop(0, count_ref.shape[0], body, jnp.int32(0))


def sigma_kernel(
    sizes,
    wide,
    c_ref,
    t_ref,
    h_ref,
    k_ref,
    count_ref,
    beta_ref,
    alpha_ref,
    cols_ref,
    z_ref,
    x_ref,
    all_ref,
    y_ref,
    sums_ref,
    b_ref,
    a_ref,
    names_ref,
    keep_ref,
    turned_ref,
    own_sem,
    back_layer_send,
    back_layer_recv,
    back_plane_send,
    back_plane_recv,
    layer_send,
    layer_recv,
    plane_send,
    plane_recv,
    cols_send,
    cols_recv,
    rise_send,
    fall_send,
    relay_recv,
    chip_send,
    chip_recv,
    pair_send,
    pair_recv,
    out_ref=None,
):
    held_ref = out_ref
    rows, cols, layers = sizes
    row, col, layer = place()
    me = row * cols + col
    step = 2 if cols % 2 == 0 else 1
    offsets = [d * cols + e for d in range(rows) for e in range(0, cols, step)]
    share, block, _ = h_ref.shape
    size = share // (rows * cols)
    half = size // 2
    square = rows == 2 and cols == 4 and half > 0

    def for_layer(i):
        return turned_ref.at[i] if wide else c_ref.at[i]

    def for_plane(i):
        if wide:
            return t_ref.at[:, pl.ds(pl.multiple_of(i * block, block), block)]
        return t_ref.at[i]

    def piece_at(piece, source):
        return all_ref.at[piece, pl.ds(pl.multiple_of(source * size, size), size)]

    greet(sizes)

    def relay(piece, up):
        mine = h_ref.at[pl.ds(pl.multiple_of(me * size, size), size)]
        src = mine if piece is None else piece_at(piece, me)
        piece = layer if piece is None else piece
        sem = rise_send if up else fall_send
        to = (row, col, layer + 1 if up else layer - 1)
        return remote(src, piece_at(piece, me), sem.at[piece], relay_recv.at[piece], to)

    def to_chip(piece, at):
        to, _ = plane_peer(sizes, row, col, offsets[at])
        return remote(
            piece_at(piece, me),
            piece_at(piece, me),
            chip_send.at[piece, at],
            chip_recv.at[piece, at],
            (*to, layer),
        )

    def to_corner(piece, part):
        _, source = plane_peer(sizes, row, col, offsets[1 + part])
        to, _ = plane_peer(sizes, row, col, offsets[2 - part])
        first = pl.multiple_of(source * size + part * half, half)
        part_ref = all_ref.at[piece, pl.ds(first, half)]
        at = 0 if part == 0 else 3
        sems = chip_send.at[piece, at], chip_recv.at[piece, at]
        return remote(part_ref, part_ref, *sems, (*to, layer))

    def to_pair(piece, at):
        _, source = plane_peer(sizes, row, col, offsets[at])
        twin = (row, col + 1 - 2 * lax.rem(col, 2), layer)
        return remote(
            piece_at(piece, source),
            piece_at(piece, source),
            pair_send.at[piece, at],
            pair_recv.at[piece, at],
            twin,
        )

    chips = [1, 2] if square else list(range(1, len(offsets)))

    def each_piece(k, act):
        @pl.when(layer >= k)
        def below():
            act(layer - k, True)

        @pl.when(layer + k < layers)
        def above():
            act(layer + k, False)

    can_rise, can_fall = layer + 1 < layers, layer > 0

    @pl.when(can_rise)
    def rise():
        relay(None, True).start()

    @pl.when(can_fall)
    def fall():
        relay(None, False).start()

    over_layer, over_plane = exchange(
        sizes, for_layer, for_plane, z_ref, x_ref, (layer_send, layer_recv, plane_send, plane_recv)
    )
    names = []
    for k in range(1, layers):
        to = (row, col, lax.rem(layer + k, layers))
        names.append(remote(k_ref, cols_ref.at[layer], cols_send.at[k], cols_recv.at[k], to))
    own = [
        pltpu.make_async_copy(for_layer(layer), z_ref.at[layer], own_sem.at[0]),
        pltpu.make_async_copy(for_plane(me), x_ref.at[me], own_sem.at[1]),
        pltpu.make_async_copy(k_ref, cols_ref.at[layer], own_sem.at[2]),
        pltpu.make_async_copy(h_ref, all_ref.at[layer], own_sem.at[3]),
    ]
    if wide:
        held = pltpu.make_async_copy(c_ref, held_ref, own_sem.at[7])
        held.start()
    for copy in names + over_plane + own[1:]:
        copy.start()
    if wide:
        held.wait()
        turn(held_ref, turned_ref)
    own[0].start()
    mark(count_ref, keep_ref, share)

    def arrive(piece, upward):
        relay(piece, upward).wait_recv()

        @pl.when(can_rise if upward else can_fall)
        def onward():
            relay(piece, upward).start()

        for at in chips:
            to_chip(piece, at).start()
        if step == 2:
            to_pair(piece, 0).start()

    def pass_on(piece, upward):
        for at in chips:
            to_chip(piece, at).wait_recv()
            if square:
                to_corner(piece, at - 1).start()
            if step == 2:
                to_pair(piece, at).start()

    def pass_corner(piece, upward):
        if square:
            to_corner(piece, 0).wait_recv()
            to_corner(piece, 1).wait_recv()
            to_pair(piece, 3).start()

    def start_layer(inner):
        for k, copy in enumerate(over_layer, 1):
            other = lax.rem(layer + k, layers)
            outer = (other == 0) | (other == layers - 1)
            pl.when(jnp.logical_not(outer) if inner else outer)(copy.start)

    early = min(2, layers - 1)
    for k in range(1, layers):
        each_piece(k, arrive)
        if k == early:
            start_layer(True)
        if k > 1 and k < layers - 1:
            each_piece(k - 1, pass_on)
    start_layer(False)
    if layers > 2:
        each_piece(layers - 2, pass_on)
    for k in range(1, layers - 2):
        each_piece(k, pass_corner)
    if layers > 1:
        each_piece(layers - 1, pass_on)
    if layers > 2:
        each_piece(layers - 2, pass_corner)

    for copy in names + over_plane + own[:3]:
        copy.wait()
    for i in range(rows * cols):
        prepare(wide, x_ref, i, y_ref, block, False)
    prepare(wide, z_ref, layer, y_ref, block, True)
    a_ref[...] = jnp.zeros_like(a_ref)
    b_ref[...] = jnp.zeros_like(b_ref)
    sums_ref[0] = jnp.zeros_like(sums_ref[0])
    to_scalars = pltpu.make_async_copy(cols_ref, names_ref, own_sem.at[4])
    to_scalars.start()
    for k, copy in enumerate(over_layer, 1):
        copy.wait()
        prepare(wide, z_ref, lax.rem(layer + layers - k, layers), y_ref, block, True)
    to_scalars.wait()
    own[3].wait()

    sign = 1 - 2 * lax.div(2 * layer, layers)

    def treat(t, carry):
        piece = lax.rem(layer + layers + t * sign, layers)

        if step == 2:

            @pl.when(t > 0)
            def complete():
                for at in range(len(offsets)):
                    to_pair(piece, at).wait_recv()

        multiply(wide, piece, all_ref, names_ref, keep_ref, y_ref, sums_ref)
        gather(wide, piece, share, count_ref, sums_ref, a_ref, b_ref)

        @pl.when(t == 0)
        def corners():
            if layers > 1:
                each_piece(layers - 1, pass_corner)

        return carry

    lax.fori_loop(0, layers, treat, 0)

    sems = (back_layer_send, back_layer_recv, back_plane_send, back_plane_recv)
    back_layer, back_plane = exchange(
        sizes, lambda i: b_ref.at[i], lambda i: a_ref.at[i], beta_ref, alpha_ref, sems
    )
    keep = [
        pltpu.make_async_copy(b_ref.at[layer], beta_ref.at[layer], own_sem.at[5]),
        pltpu.make_async_copy(a_ref.at[me], alpha_ref.at[me], own_sem.at[6]),
    ]
    for copy in back_layer + back_plane + keep:
        copy.start()

    def finish(piece, upward):
        @pl.when(can_rise if upward else can_fall)
        def sent():
            relay(piece, upward).wait_send()

        for at in chips:
            to_chip(piece, at).wait_send()
        if square:
            to_corner(piece, 0).wait_send()
            to_corner(piece, 1).wait_send()
        if step == 2:
            for at in range(len(offsets)):
                to_pair(piece, at).wait_send()

    for k in range(1, layers):
        each_piece(k, finish)

    @pl.when(can_rise)
    def risen():
        relay(None, True).wait_send()

    @pl.when(can_fall)
    def fallen():
        relay(None, False).wait_send()

    for copy in back_plane + keep:
        copy.wait()

    def join(i):
        for p in range(rows * cols):
            at = pl.ds(pl.multiple_of(i * block, block), block)
            out_ref[at, p * block : (p + 1) * block] = beta_ref[i, p].T + alpha_ref[p, i]

    if wide:
        join(layer)
    for k, copy in enumerate(back_layer, 1):
        copy.wait()
        if wide:
            join(lax.rem(layer + layers - k, layers))


def wide_kernel(sizes, c, t, h, k, count, out_ref, columns, beta, alpha, *scratch):
    sigma_kernel(sizes, True, c, t, h, k, count, beta, alpha, columns, *scratch, out_ref=out_ref)


def local(sizes, coeffs, hblocks, hcount, hcols):
    rows, cols, layers = sizes
    group = rows * cols
    row_count, col_count = coeffs.shape
    share, block, _ = hblocks.shape
    stored = share * layers
    blocks = row_count * group // block
    alpha_rows, beta_rows = col_count // group, row_count // layers
    per_layer, per_plane = blocks // layers, blocks // group
    beta_back = (layers, per_layer, beta_rows, block)
    alpha_back = (group, per_plane, alpha_rows, block)
    f32 = jnp.float32
    dma = pltpu.SemaphoreType.DMA

    wide = alpha_rows == block and beta_rows == block
    names = hcols.reshape(1, share)
    if wide:
        for_layer, for_plane = coeffs, coeffs
        z_shape, x_shape = (layers, col_count, block), (group, row_count, block)
        y_shape, sum_shape = (blocks, 2 * block, 2 * block), (share + 1, block, 2 * block)
        turned = z_shape
    else:
        for_layer = coeffs.reshape(layers, beta_rows, col_count)
        for_plane = coeffs.T.reshape(group, alpha_rows, row_count)
        z_shape, x_shape = for_layer.shape, for_plane.shape
        both = alpha_rows + beta_rows
        y_shape, sum_shape = (blocks, both, 2 * block), (share + 1, both, block)
        turned = (8, 128)
    chips = group // 2 if cols % 2 == 0 else group
    smem = pl.BlockSpec(memory_space=pltpu.SMEM)
    gathered = jax.ShapeDtypeStruct((layers, *names.shape), jnp.int32)
    if wide:
        kernel = functools.partial(wide_kernel, sizes)
        out_shape = (jax.ShapeDtypeStruct((row_count, col_count), f32), gathered)
        out_specs = (pl.BlockSpec(memory_space=pltpu.VMEM), ANY)
        landing = [pltpu.VMEM(beta_back, f32), pltpu.VMEM(alpha_back, f32)]
    else:
        kernel = functools.partial(sigma_kernel, sizes, False)
        out_shape = (
            jax.ShapeDtypeStruct(beta_back, f32),
            jax.ShapeDtypeStruct(alpha_back, f32),
            gathered,
        )
        out_specs = (ANY,) * 3
        landing = []
    results = pl.pallas_call(
        kernel,
        out_shape=out_shape,
        in_specs=[ANY] * 4 + [smem],
        out_specs=out_specs,
        scratch_shapes=landing
        + [
            pltpu.VMEM(z_shape, f32),
            pltpu.VMEM(x_shape, f32),
            pltpu.VMEM((layers, share, block, block), f32),
            pltpu.VMEM(y_shape, jnp.bfloat16),
            pltpu.VMEM(sum_shape, f32),
            pltpu.VMEM(beta_back, f32),
            pltpu.VMEM(alpha_back, f32),
            pltpu.SMEM((layers, *names.shape), jnp.int32),
            pltpu.SMEM((stored,), f32),
            pltpu.VMEM(turned, f32),
            dma((8,)),
        ]
        + ([dma((layers,))] * 2 + [dma((group,))] * 2) * 2
        + [dma((layers,))] * 5
        + [dma((layers, chips))] * 4,
        compiler_params=pltpu.CompilerParams(
            collective_id=0, has_side_effects=True, vmem_limit_bytes=48 * 2**20
        ),
        name="sigma",
    )(
        for_layer,
        for_plane,
        hblocks,
        names,
        hcount,
    )
    if wide:
        return results[0]
    beta, alpha, _ = results
    beta = beta.transpose(0, 2, 1, 3).reshape(row_count, col_count)
    alpha = alpha.transpose(1, 3, 0, 2).reshape(row_count, col_count)
    return beta + alpha


def solution(mesh):
    sizes = tuple(mesh.shape[name] for name in ("row", "col", "layer"))
    in_specs = (P(("row", "col"), "layer"), P("layer", None, None), P(), P("layer"))
    out_specs = P(("row", "col"), "layer")
    return jax.shard_map(
        functools.partial(local, sizes),
        mesh=mesh,
        in_specs=in_specs,
        out_specs=out_specs,
        check_vma=False,
    )
```

```python
import functools

import jax
import jax.numpy as jnp
from jax import lax
from jax.experimental import pallas as pl
from jax.experimental.pallas import tpu as pltpu
from jax.sharding import PartitionSpec as P

MESH = pl.DeviceIdType.MESH
ANY = pl.BlockSpec(memory_space=pl.ANY)


def place():
    return lax.axis_index("row"), lax.axis_index("col"), lax.axis_index("layer")


def plane_peer(sizes, row, col, offset):
    rows, cols, _ = sizes
    down, right = offset // cols, offset % cols
    to = (lax.rem(row + down, rows), lax.rem(col + right, cols))
    source = lax.rem(row + rows - down, rows) * cols + lax.rem(col + cols - right, cols)
    return to, source


def greet(sizes):
    rows, cols, layers = sizes
    row, col, layer = place()
    barrier = pltpu.get_barrier_semaphore()
    for k in range(1, layers):
        to = (row, col, lax.rem(layer + k, layers))
        pl.semaphore_signal(barrier, inc=1, device_id=to, device_id_type=MESH)
    for offset in range(1, rows * cols):
        to, _ = plane_peer(sizes, row, col, offset)
        pl.semaphore_signal(barrier, inc=1, device_id=(*to, layer), device_id_type=MESH)
    pl.semaphore_wait(barrier, layers - 1 + rows * cols - 1)


def remote(src, dst, send_sem, recv_sem, to):
    return pltpu.make_async_remote_copy(
        src_ref=src,
        dst_ref=dst,
        send_sem=send_sem,
        recv_sem=recv_sem,
        device_id=to,
        device_id_type=MESH,
    )


def exchange(sizes, by_layer, by_plane, to_layer, to_plane, sems):
    rows, cols, layers = sizes
    row, col, layer = place()
    layer_send, layer_recv, plane_send, plane_recv = sems
    over_layer, over_plane = [], []
    for k in range(1, layers):
        other = lax.rem(layer + k, layers)
        over_layer.append(
            remote(
                by_layer(other),
                to_layer.at[layer],
                layer_send.at[k],
                layer_recv.at[k],
                (row, col, other),
            )
        )
    me = row * cols + col
    for offset in range(1, rows * cols):
        to, _ = plane_peer(sizes, row, col, offset)
        over_plane.append(
            remote(
                by_plane(to[0] * cols + to[1]),
                to_plane.at[me],
                plane_send.at[offset],
                plane_recv.at[offset],
                (*to, layer),
            )
        )
    return over_layer, over_plane


def halves(values):
    high = values.astype(jnp.bfloat16)
    low = (values - high.astype(jnp.float32)).astype(jnp.bfloat16)
    return high, low


def turn(held_ref, turned_ref):
    layers, width, block = turned_ref.shape
    for i in range(layers):
        for j in range(width // block):
            part = held_ref[i * block : (i + 1) * block, j * block : (j + 1) * block]
            turned_ref[i, j * block : (j + 1) * block, :] = part.T


def mark(count_ref, keep_ref, share):
    blocks = count_ref.shape[0]

    def body(n, carry):
        row, end = carry
        opens = n == end
        row = jnp.minimum(jnp.where(opens, row + 1, row), blocks - 1)
        end = jnp.where(opens, end + count_ref[row], end)
        keep_ref[n] = jnp.where(opens | (lax.rem(n, share) == 0), 0.0, 1.0)
        return row, end

    lax.fori_loop(0, keep_ref.shape[0], body, (jnp.int32(0), count_ref[0]))


def prepare(wide, ref, i, y_ref, block, beta):
    if wide:
        per = ref.shape[1] // block
        side = slice(block, 2 * block) if beta else slice(0, block)
        for j in range(per):
            high, low = halves(ref[i, j * block : (j + 1) * block, :])
            y_ref[i * per + j, :block, side] = high
            y_ref[i * per + j, block:, side] = low
        return
    per, count = ref.shape[2] // block, ref.shape[1]
    first = y_ref.shape[1] - count if beta else 0
    for j in range(per):
        high, low = halves(ref[i, :, j * block : (j + 1) * block])
        y_ref[i * per + j, first : first + count, :block] = high
        y_ref[i * per + j, first : first + count, block:] = low


def lanes_of(side, block):
    return {"alpha": slice(0, block), "beta": slice(block, 2 * block), "both": slice(None)}[side]


def multiply(wide, side, piece, all_ref, names_ref, keep_ref, y_ref, sums_ref):
    _, share, block, _ = all_ref.shape
    group = 8 if share % 8 == 0 else 1
    lanes = lanes_of(side, block)

    def body(at, carry):
        running = sums_ref[at * group, :, lanes]
        for i in range(group):
            n = at * group + i
            high, low = halves(all_ref[piece, n])
            four = jnp.concatenate(
                [jnp.concatenate([high, high], axis=1), jnp.concatenate([low, low], axis=1)], axis=0
            )
            picked = y_ref[names_ref[piece, 0, n], :, lanes]
            if wide:
                both = jnp.dot(four, picked, preferred_element_type=jnp.float32)
                result = both[:block] + both[block:]
            else:
                both = lax.dot_general(
                    picked, four, (((1,), (1,)), ((), ())), preferred_element_type=jnp.float32
                )
                result = both[:, :block] + both[:, block:]
            running = result + keep_ref[piece * share + n] * running
            sums_ref[n + 1, :, lanes] = running
        return carry

    lax.fori_loop(0, share // group, body, 0)


def gather(wide, side, piece, share, count_ref, sums_ref, a_ref, b_ref):
    alpha_rows, block = a_ref.shape[2:]
    per_a, per_b = a_ref.shape[1], b_ref.shape[1]
    base = piece * share

    def body(i, start):
        end = start + count_ref[i]
        low, high = jnp.maximum(start, base), jnp.minimum(end, base + share)
        found = jnp.where(high > low, 1.0, 0.0)
        part = found * sums_ref[jnp.clip(high - base, 1, share), :, lanes_of(side, block)]
        if side != "both":
            for_a = for_b = part
        elif wide:
            for_a, for_b = part[:, :block], part[:, block:]
        else:
            for_a, for_b = part[:alpha_rows], part[alpha_rows:]
        if side != "beta":
            a_ref[lax.div(i, per_a), lax.rem(i, per_a)] += for_a
        if side != "alpha":
            b_ref[lax.div(i, per_b), lax.rem(i, per_b)] += for_b
        return end

    lax.fori_loop(0, count_ref.shape[0], body, jnp.int32(0))


def sigma_kernel(
    sizes,
    wide,
    c_ref,
    t_ref,
    h_ref,
    k_ref,
    count_ref,
    beta_ref,
    alpha_ref,
    cols_ref,
    z_ref,
    x_ref,
    all_ref,
    y_ref,
    sums_ref,
    b_ref,
    a_ref,
    names_ref,
    keep_ref,
    held_ref,
    turned_ref,
    own_sem,
    back_layer_send,
    back_layer_recv,
    back_plane_send,
    back_plane_recv,
    layer_send,
    layer_recv,
    plane_send,
    plane_recv,
    cols_send,
    cols_recv,
    rise_send,
    fall_send,
    relay_recv,
    chip_send,
    chip_recv,
    pair_send,
    pair_recv,
    out_ref=None,
):
    rows, cols, layers = sizes
    row, col, layer = place()
    me = row * cols + col
    step = 2 if cols % 2 == 0 else 1
    offsets = [d * cols + e for d in range(rows) for e in range(0, cols, step)]
    share, block, _ = h_ref.shape
    size = share // (rows * cols)
    half = size // 2
    square = rows == 2 and cols == 4 and half > 0

    def for_layer(i):
        return turned_ref.at[i] if wide else c_ref.at[i]

    def for_plane(i):
        if wide:
            return t_ref.at[:, pl.ds(pl.multiple_of(i * block, block), block)]
        return t_ref.at[i]

    def piece_at(piece, source):
        return all_ref.at[piece, pl.ds(pl.multiple_of(source * size, size), size)]

    greet(sizes)

    def relay(piece, up):
        mine = h_ref.at[pl.ds(pl.multiple_of(me * size, size), size)]
        src = mine if piece is None else piece_at(piece, me)
        piece = layer if piece is None else piece
        sem = rise_send if up else fall_send
        to = (row, col, layer + 1 if up else layer - 1)
        return remote(src, piece_at(piece, me), sem.at[piece], relay_recv.at[piece], to)

    def to_chip(piece, at):
        to, _ = plane_peer(sizes, row, col, offsets[at])
        return remote(
            piece_at(piece, me),
            piece_at(piece, me),
            chip_send.at[piece, at],
            chip_recv.at[piece, at],
            (*to, layer),
        )

    def to_corner(piece, part):
        _, source = plane_peer(sizes, row, col, offsets[1 + part])
        to, _ = plane_peer(sizes, row, col, offsets[2 - part])
        first = pl.multiple_of(source * size + part * half, half)
        part_ref = all_ref.at[piece, pl.ds(first, half)]
        at = 0 if part == 0 else 3
        sems = chip_send.at[piece, at], chip_recv.at[piece, at]
        return remote(part_ref, part_ref, *sems, (*to, layer))

    def to_pair(piece, at):
        _, source = plane_peer(sizes, row, col, offsets[at])
        twin = (row, col + 1 - 2 * lax.rem(col, 2), layer)
        return remote(
            piece_at(piece, source),
            piece_at(piece, source),
            pair_send.at[piece, at],
            pair_recv.at[piece, at],
            twin,
        )

    chips = [1, 2] if square else list(range(1, len(offsets)))

    def each_piece(k, act):
        @pl.when(layer >= k)
        def below():
            act(layer - k, True)

        @pl.when(layer + k < layers)
        def above():
            act(layer + k, False)

    can_rise, can_fall = layer + 1 < layers, layer > 0

    @pl.when(can_rise)
    def rise():
        relay(None, True).start()

    @pl.when(can_fall)
    def fall():
        relay(None, False).start()

    over_layer, over_plane = exchange(
        sizes, for_layer, for_plane, z_ref, x_ref, (layer_send, layer_recv, plane_send, plane_recv)
    )
    names = []
    for k in range(1, layers):
        to = (row, col, lax.rem(layer + k, layers))
        names.append(remote(k_ref, cols_ref.at[layer], cols_send.at[k], cols_recv.at[k], to))
    own = [
        pltpu.make_async_copy(for_layer(layer), z_ref.at[layer], own_sem.at[0]),
        pltpu.make_async_copy(for_plane(me), x_ref.at[me], own_sem.at[1]),
        pltpu.make_async_copy(k_ref, cols_ref.at[layer], own_sem.at[2]),
        pltpu.make_async_copy(h_ref, all_ref.at[layer], own_sem.at[3]),
    ]
    if wide:
        held = pltpu.make_async_copy(c_ref, held_ref, own_sem.at[7])
        held.start()
    for copy in names + over_plane + own[1:]:
        copy.start()
    if wide:
        held.wait()
        turn(held_ref, turned_ref)
    own[0].start()
    mark(count_ref, keep_ref, share)

    def arrive(piece, upward):
        relay(piece, upward).wait_recv()

        @pl.when(can_rise if upward else can_fall)
        def onward():
            relay(piece, upward).start()

        for at in chips:
            to_chip(piece, at).start()
        if step == 2:
            to_pair(piece, 0).start()

    def pass_on(piece, upward):
        for at in chips:
            to_chip(piece, at).wait_recv()
            if square:
                to_corner(piece, at - 1).start()
            if step == 2:
                to_pair(piece, at).start()

    def pass_corner(piece, upward):
        if square:
            to_corner(piece, 0).wait_recv()
            to_corner(piece, 1).wait_recv()
            to_pair(piece, 3).start()

    early = 1
    for k in range(1, layers):
        each_piece(k, arrive)
        if k == early:
            for copy in over_layer:
                copy.start()
        if k > 1 and k < layers - 1:
            each_piece(k - 1, pass_on)
    if layers > 2:
        each_piece(layers - 2, pass_on)
    for k in range(1, layers - 2):
        each_piece(k, pass_corner)
    if layers > 1:
        each_piece(layers - 1, pass_on)
    if layers > 2:
        each_piece(layers - 2, pass_corner)

    for copy in names + over_plane + own[:3]:
        copy.wait()
    for i in range(rows * cols):
        prepare(wide, x_ref, i, y_ref, block, False)
    prepare(wide, z_ref, layer, y_ref, block, True)
    a_ref[...] = jnp.zeros_like(a_ref)
    b_ref[...] = jnp.zeros_like(b_ref)
    sums_ref[0] = jnp.zeros_like(sums_ref[0])
    to_scalars = pltpu.make_async_copy(cols_ref, names_ref, own_sem.at[4])
    to_scalars.start()
    to_scalars.wait()
    own[3].wait()
    sign = 1 - 2 * lax.div(2 * layer, layers)

    def piece_of(t):
        return lax.rem(layer + layers + t * sign, layers)

    def complete(t):
        if step == 2:
            for at in range(len(offsets)):
                to_pair(piece_of(t), at).wait_recv()

    def work(t, side):
        piece = piece_of(t)
        multiply(wide, side, piece, all_ref, names_ref, keep_ref, y_ref, sums_ref)
        gather(wide, side, piece, share, count_ref, sums_ref, a_ref, b_ref)

    ahead = 2 if wide and layers > 2 else 0
    for t in range(ahead):
        if t > 0:
            complete(t)
        work(t, "alpha")
    for k, copy in enumerate(over_layer, 1):
        copy.wait()
        prepare(wide, z_ref, lax.rem(layer + layers - k, layers), y_ref, block, True)
    work(0, "beta" if ahead > 0 else "both")
    if layers > 1:
        each_piece(layers - 1, pass_corner)
    if ahead > 1:
        work(1, "beta")

    def treat(t, carry):
        complete(t)
        work(t, "both")
        return carry

    lax.fori_loop(max(1, ahead), layers, treat, 0)

    sems = (back_layer_send, back_layer_recv, back_plane_send, back_plane_recv)
    back_layer, back_plane = exchange(
        sizes, lambda i: b_ref.at[i], lambda i: a_ref.at[i], beta_ref, alpha_ref, sems
    )
    keep = [
        pltpu.make_async_copy(b_ref.at[layer], beta_ref.at[layer], own_sem.at[5]),
        pltpu.make_async_copy(a_ref.at[me], alpha_ref.at[me], own_sem.at[6]),
    ]
    for copy in back_layer + back_plane + keep:
        copy.start()

    def finish(piece, upward):
        @pl.when(can_rise if upward else can_fall)
        def sent():
            relay(piece, upward).wait_send()

        for at in chips:
            to_chip(piece, at).wait_send()
        if square:
            to_corner(piece, 0).wait_send()
            to_corner(piece, 1).wait_send()
        if step == 2:
            for at in range(len(offsets)):
                to_pair(piece, at).wait_send()

    for k in range(1, layers):
        each_piece(k, finish)

    @pl.when(can_rise)
    def risen():
        relay(None, True).wait_send()

    @pl.when(can_fall)
    def fallen():
        relay(None, False).wait_send()

    for copy in back_plane + keep:
        copy.wait()

    def join(i):
        for p in range(rows * cols):
            at = pl.ds(pl.multiple_of(i * block, block), block)
            out_ref[at, p * block : (p + 1) * block] = beta_ref[i, p].T + alpha_ref[p, i]

    if wide:
        join(layer)
    for k, copy in enumerate(back_layer, 1):
        copy.wait()
        if wide:
            join(lax.rem(layer + layers - k, layers))


def wide_kernel(sizes, c, t, h, k, count, out_ref, columns, beta, alpha, *scratch):
    sigma_kernel(sizes, True, c, t, h, k, count, beta, alpha, columns, *scratch, out_ref=out_ref)


def local(sizes, coeffs, hblocks, hcount, hcols):
    rows, cols, layers = sizes
    group = rows * cols
    row_count, col_count = coeffs.shape
    share, block, _ = hblocks.shape
    stored = share * layers
    blocks = row_count * group // block
    alpha_rows, beta_rows = col_count // group, row_count // layers
    per_layer, per_plane = blocks // layers, blocks // group
    beta_back = (layers, per_layer, beta_rows, block)
    alpha_back = (group, per_plane, alpha_rows, block)
    f32 = jnp.float32
    dma = pltpu.SemaphoreType.DMA

    wide = alpha_rows == block and beta_rows == block
    names = hcols.reshape(1, share)
    if wide:
        for_layer, for_plane = coeffs, coeffs
        z_shape, x_shape = (layers, col_count, block), (group, row_count, block)
        y_shape, sum_shape = (blocks, 2 * block, 2 * block), (share + 1, block, 2 * block)
        held, turned = coeffs.shape, z_shape
    else:
        for_layer = coeffs.reshape(layers, beta_rows, col_count)
        for_plane = coeffs.T.reshape(group, alpha_rows, row_count)
        z_shape, x_shape = for_layer.shape, for_plane.shape
        both = alpha_rows + beta_rows
        y_shape, sum_shape = (blocks, both, 2 * block), (share + 1, both, block)
        held = turned = (8, 128)
    chips = group // 2 if cols % 2 == 0 else group
    smem = pl.BlockSpec(memory_space=pltpu.SMEM)
    gathered = jax.ShapeDtypeStruct((layers, *names.shape), jnp.int32)
    if wide:
        kernel = functools.partial(wide_kernel, sizes)
        out_shape = (jax.ShapeDtypeStruct((row_count, col_count), f32), gathered)
        out_specs = (pl.BlockSpec(memory_space=pltpu.VMEM), ANY)
        landing = [pltpu.VMEM(beta_back, f32), pltpu.VMEM(alpha_back, f32)]
    else:
        kernel = functools.partial(sigma_kernel, sizes, False)
        out_shape = (
            jax.ShapeDtypeStruct(beta_back, f32),
            jax.ShapeDtypeStruct(alpha_back, f32),
            gathered,
        )
        out_specs = (ANY,) * 3
        landing = []
    results = pl.pallas_call(
        kernel,
        out_shape=out_shape,
        in_specs=[ANY] * 4 + [smem],
        out_specs=out_specs,
        scratch_shapes=landing
        + [
            pltpu.VMEM(z_shape, f32),
            pltpu.VMEM(x_shape, f32),
            pltpu.VMEM((layers, share, block, block), f32),
            pltpu.VMEM(y_shape, jnp.bfloat16),
            pltpu.VMEM(sum_shape, f32),
            pltpu.VMEM(beta_back, f32),
            pltpu.VMEM(alpha_back, f32),
            pltpu.SMEM((layers, *names.shape), jnp.int32),
            pltpu.SMEM((stored,), f32),
            pltpu.VMEM(held, f32),
            pltpu.VMEM(turned, f32),
            dma((8,)),
        ]
        + ([dma((layers,))] * 2 + [dma((group,))] * 2) * 2
        + [dma((layers,))] * 5
        + [dma((layers, chips))] * 4,
        compiler_params=pltpu.CompilerParams(
            collective_id=0, has_side_effects=True, vmem_limit_bytes=56 * 2**20
        ),
        name="sigma",
    )(
        for_layer,
        for_plane,
        hblocks,
        names,
        hcount,
    )
    if wide:
        return results[0]
    beta, alpha, _ = results
    beta = beta.transpose(0, 2, 1, 3).reshape(row_count, col_count)
    alpha = alpha.transpose(1, 3, 0, 2).reshape(row_count, col_count)
    return beta + alpha


def solution(mesh):
    sizes = tuple(mesh.shape[name] for name in ("row", "col", "layer"))
    in_specs = (P(("row", "col"), "layer"), P("layer", None, None), P(), P("layer"))
    out_specs = P(("row", "col"), "layer")
    return jax.shard_map(
        functools.partial(local, sizes),
        mesh=mesh,
        in_specs=in_specs,
        out_specs=out_specs,
        check_vma=False,
    )
```

```python
import functools

import jax
import jax.numpy as jnp
from jax import lax
from jax.experimental import pallas as pl
from jax.experimental.pallas import tpu as pltpu
from jax.sharding import PartitionSpec as P

MESH = pl.DeviceIdType.MESH
ANY = pl.BlockSpec(memory_space=pl.ANY)


def place():
    return lax.axis_index("row"), lax.axis_index("col"), lax.axis_index("layer")


def plane_peer(sizes, row, col, offset):
    rows, cols, _ = sizes
    down, right = offset // cols, offset % cols
    to = (lax.rem(row + down, rows), lax.rem(col + right, cols))
    source = lax.rem(row + rows - down, rows) * cols + lax.rem(col + cols - right, cols)
    return to, source


def greet(sizes):
    rows, cols, layers = sizes
    row, col, layer = place()
    barrier = pltpu.get_barrier_semaphore()
    for k in range(1, layers):
        to = (row, col, lax.rem(layer + k, layers))
        pl.semaphore_signal(barrier, inc=1, device_id=to, device_id_type=MESH)
    for offset in range(1, rows * cols):
        to, _ = plane_peer(sizes, row, col, offset)
        pl.semaphore_signal(barrier, inc=1, device_id=(*to, layer), device_id_type=MESH)
    pl.semaphore_wait(barrier, layers - 1 + rows * cols - 1)


def remote(src, dst, send_sem, recv_sem, to):
    return pltpu.make_async_remote_copy(
        src_ref=src,
        dst_ref=dst,
        send_sem=send_sem,
        recv_sem=recv_sem,
        device_id=to,
        device_id_type=MESH,
    )


def exchange(sizes, by_layer, by_plane, to_layer, to_plane, sems):
    rows, cols, layers = sizes
    row, col, layer = place()
    layer_send, layer_recv, plane_send, plane_recv = sems
    over_layer, over_plane = [], []
    for k in range(1, layers):
        other = lax.rem(layer + k, layers)
        over_layer.append(
            remote(
                by_layer(other),
                to_layer.at[layer],
                layer_send.at[k],
                layer_recv.at[k],
                (row, col, other),
            )
        )
    me = row * cols + col
    for offset in range(1, rows * cols):
        to, _ = plane_peer(sizes, row, col, offset)
        over_plane.append(
            remote(
                by_plane(to[0] * cols + to[1]),
                to_plane.at[me],
                plane_send.at[offset],
                plane_recv.at[offset],
                (*to, layer),
            )
        )
    return over_layer, over_plane


def halves(values):
    high = values.astype(jnp.bfloat16)
    low = (values - high.astype(jnp.float32)).astype(jnp.bfloat16)
    return high, low


def turn(held_ref, turned_ref):
    layers, width, block = turned_ref.shape
    for i in range(layers):
        for j in range(width // block):
            part = held_ref[i * block : (i + 1) * block, j * block : (j + 1) * block]
            turned_ref[i, j * block : (j + 1) * block, :] = part.T


def mark(count_ref, keep_ref, share):
    blocks = count_ref.shape[0]

    def body(n, carry):
        row, end = carry
        opens = n == end
        row = jnp.minimum(jnp.where(opens, row + 1, row), blocks - 1)
        end = jnp.where(opens, end + count_ref[row], end)
        keep_ref[n] = jnp.where(opens | (lax.rem(n, share) == 0), 0.0, 1.0)
        return row, end

    lax.fori_loop(0, keep_ref.shape[0], body, (jnp.int32(0), count_ref[0]))


def prepare(wide, ref, i, y_ref, block, beta):
    if wide:
        per = ref.shape[1] // block
        side = slice(block, 2 * block) if beta else slice(0, block)
        for j in range(per):
            high, low = halves(ref[i, j * block : (j + 1) * block, :])
            y_ref[i * per + j, :block, side] = high
            y_ref[i * per + j, block:, side] = low
        return
    per, count = ref.shape[2] // block, ref.shape[1]
    first = y_ref.shape[1] - count if beta else 0
    for j in range(per):
        high, low = halves(ref[i, :, j * block : (j + 1) * block])
        y_ref[i * per + j, first : first + count, :block] = high
        y_ref[i * per + j, first : first + count, block:] = low


def lanes_of(side, block):
    return {"alpha": slice(0, block), "beta": slice(block, 2 * block), "both": slice(None)}[side]


def multiply(wide, side, piece, all_ref, names_ref, keep_ref, y_ref, sums_ref):
    _, share, block, _ = all_ref.shape
    group = 8 if share % 8 == 0 else 1
    lanes = lanes_of(side, block)

    def body(at, carry):
        running = sums_ref[at * group, :, lanes]
        for i in range(group):
            n = at * group + i
            high, low = halves(all_ref[piece, n])
            four = jnp.concatenate(
                [jnp.concatenate([high, high], axis=1), jnp.concatenate([low, low], axis=1)], axis=0
            )
            picked = y_ref[names_ref[piece, 0, n], :, lanes]
            if wide:
                both = jnp.dot(four, picked, preferred_element_type=jnp.float32)
                result = both[:block] + both[block:]
            else:
                both = lax.dot_general(
                    picked, four, (((1,), (1,)), ((), ())), preferred_element_type=jnp.float32
                )
                result = both[:, :block] + both[:, block:]
            running = result + keep_ref[piece * share + n] * running
            sums_ref[n + 1, :, lanes] = running
        return carry

    lax.fori_loop(0, share // group, body, 0)


def gather(wide, side, piece, share, count_ref, sums_ref, a_ref, b_ref):
    alpha_rows, block = a_ref.shape[2:]
    per_a, per_b = a_ref.shape[1], b_ref.shape[1]
    base = piece * share

    def body(i, start):
        end = start + count_ref[i]
        low, high = jnp.maximum(start, base), jnp.minimum(end, base + share)
        found = jnp.where(high > low, 1.0, 0.0)
        part = found * sums_ref[jnp.clip(high - base, 1, share), :, lanes_of(side, block)]
        if side != "both":
            for_a = for_b = part
        elif wide:
            for_a, for_b = part[:, :block], part[:, block:]
        else:
            for_a, for_b = part[:alpha_rows], part[alpha_rows:]
        if side != "beta":
            a_ref[lax.div(i, per_a), lax.rem(i, per_a)] += for_a
        if side != "alpha":
            b_ref[lax.div(i, per_b), lax.rem(i, per_b)] += for_b
        return end

    lax.fori_loop(0, count_ref.shape[0], body, jnp.int32(0))


def sigma_kernel(
    sizes,
    wide,
    c_ref,
    t_ref,
    h_ref,
    k_ref,
    count_ref,
    beta_ref,
    alpha_ref,
    cols_ref,
    z_ref,
    x_ref,
    all_ref,
    y_ref,
    sums_ref,
    b_ref,
    a_ref,
    names_ref,
    keep_ref,
    held_ref,
    turned_ref,
    own_sem,
    back_layer_send,
    back_layer_recv,
    back_plane_send,
    back_plane_recv,
    layer_send,
    layer_recv,
    plane_send,
    plane_recv,
    cols_send,
    cols_recv,
    rise_send,
    fall_send,
    relay_recv,
    chip_send,
    chip_recv,
    pair_send,
    pair_recv,
    out_ref=None,
):
    rows, cols, layers = sizes
    row, col, layer = place()
    me = row * cols + col
    step = 2 if cols % 2 == 0 else 1
    offsets = [d * cols + e for d in range(rows) for e in range(0, cols, step)]
    share, block, _ = h_ref.shape
    size = share // (rows * cols)
    half = size // 2
    square = rows == 2 and cols == 4 and half > 0

    def for_layer(i):
        return turned_ref.at[i] if wide else c_ref.at[i]

    def for_plane(i):
        if wide:
            return t_ref.at[:, pl.ds(pl.multiple_of(i * block, block), block)]
        return t_ref.at[i]

    def piece_at(piece, source):
        return all_ref.at[piece, pl.ds(pl.multiple_of(source * size, size), size)]

    greet(sizes)

    def relay(piece, up):
        mine = h_ref.at[pl.ds(pl.multiple_of(me * size, size), size)]
        src = mine if piece is None else piece_at(piece, me)
        piece = layer if piece is None else piece
        sem = rise_send if up else fall_send
        to = (row, col, layer + 1 if up else layer - 1)
        return remote(src, piece_at(piece, me), sem.at[piece], relay_recv.at[piece], to)

    def to_chip(piece, at):
        to, _ = plane_peer(sizes, row, col, offsets[at])
        return remote(
            piece_at(piece, me),
            piece_at(piece, me),
            chip_send.at[piece, at],
            chip_recv.at[piece, at],
            (*to, layer),
        )

    def to_corner(piece, part):
        _, source = plane_peer(sizes, row, col, offsets[1 + part])
        to, _ = plane_peer(sizes, row, col, offsets[2 - part])
        first = pl.multiple_of(source * size + part * half, half)
        part_ref = all_ref.at[piece, pl.ds(first, half)]
        at = 0 if part == 0 else 3
        sems = chip_send.at[piece, at], chip_recv.at[piece, at]
        return remote(part_ref, part_ref, *sems, (*to, layer))

    def to_pair(piece, at):
        _, source = plane_peer(sizes, row, col, offsets[at])
        twin = (row, col + 1 - 2 * lax.rem(col, 2), layer)
        return remote(
            piece_at(piece, source),
            piece_at(piece, source),
            pair_send.at[piece, at],
            pair_recv.at[piece, at],
            twin,
        )

    chips = [1, 2] if square else list(range(1, len(offsets)))

    def each_piece(k, act):
        @pl.when(layer >= k)
        def below():
            act(layer - k, True)

        @pl.when(layer + k < layers)
        def above():
            act(layer + k, False)

    can_rise, can_fall = layer + 1 < layers, layer > 0

    @pl.when(can_rise)
    def rise():
        relay(None, True).start()

    @pl.when(can_fall)
    def fall():
        relay(None, False).start()

    over_layer, over_plane = exchange(
        sizes, for_layer, for_plane, z_ref, x_ref, (layer_send, layer_recv, plane_send, plane_recv)
    )
    names = []
    for k in range(1, layers):
        to = (row, col, lax.rem(layer + k, layers))
        names.append(remote(k_ref, cols_ref.at[layer], cols_send.at[k], cols_recv.at[k], to))
    own = [
        pltpu.make_async_copy(for_layer(layer), z_ref.at[layer], own_sem.at[0]),
        pltpu.make_async_copy(for_plane(me), x_ref.at[me], own_sem.at[1]),
        pltpu.make_async_copy(k_ref, cols_ref.at[layer], own_sem.at[2]),
        pltpu.make_async_copy(h_ref, all_ref.at[layer], own_sem.at[3]),
    ]
    if wide:
        held = pltpu.make_async_copy(c_ref, held_ref, own_sem.at[7])
        held.start()
    for copy in names + over_plane + own[1:]:
        copy.start()
    if wide:
        held.wait()
        turn(held_ref, turned_ref)
    own[0].start()
    mark(count_ref, keep_ref, share)

    def arrive(piece, upward):
        relay(piece, upward).wait_recv()

        @pl.when(can_rise if upward else can_fall)
        def onward():
            relay(piece, upward).start()

        for at in chips:
            to_chip(piece, at).start()
        if step == 2:
            to_pair(piece, 0).start()

    def pass_on(piece, upward):
        for at in chips:
            to_chip(piece, at).wait_recv()
            if square:
                to_corner(piece, at - 1).start()
            if step == 2:
                to_pair(piece, at).start()

    def pass_corner(piece, upward):
        if square:
            to_corner(piece, 0).wait_recv()
            to_corner(piece, 1).wait_recv()
            to_pair(piece, 3).start()

    early = min(2, layers - 1)
    for k in range(1, layers):
        each_piece(k, arrive)
        if k == early:
            for copy in over_layer:
                copy.start()
        if k > 1 and k < layers - 1:
            each_piece(k - 1, pass_on)
    if layers > 2:
        each_piece(layers - 2, pass_on)
    for k in range(1, layers - 2):
        each_piece(k, pass_corner)
    if layers > 1:
        each_piece(layers - 1, pass_on)
    if layers > 2:
        each_piece(layers - 2, pass_corner)

    for copy in names + over_plane + own[:3]:
        copy.wait()
    for i in range(rows * cols):
        prepare(wide, x_ref, i, y_ref, block, False)
    prepare(wide, z_ref, layer, y_ref, block, True)
    a_ref[...] = jnp.zeros_like(a_ref)
    b_ref[...] = jnp.zeros_like(b_ref)
    sums_ref[0] = jnp.zeros_like(sums_ref[0])
    to_scalars = pltpu.make_async_copy(cols_ref, names_ref, own_sem.at[4])
    to_scalars.start()
    to_scalars.wait()
    own[3].wait()
    sign = 1 - 2 * lax.div(2 * layer, layers)

    def piece_of(t):
        return lax.rem(layer + layers + t * sign, layers)

    def complete(t):
        if step == 2:
            for at in range(len(offsets)):
                to_pair(piece_of(t), at).wait_recv()

    def work(t, side):
        piece = piece_of(t)
        multiply(wide, side, piece, all_ref, names_ref, keep_ref, y_ref, sums_ref)
        gather(wide, side, piece, share, count_ref, sums_ref, a_ref, b_ref)

    ahead = 1 if wide else 0
    for t in range(ahead):
        if t > 0:
            complete(t)
        work(t, "alpha")
    for k, copy in enumerate(over_layer, 1):
        copy.wait()
        prepare(wide, z_ref, lax.rem(layer + layers - k, layers), y_ref, block, True)
    work(0, "beta" if ahead > 0 else "both")
    if layers > 1:
        each_piece(layers - 1, pass_corner)
    if ahead > 1:
        work(1, "beta")

    def treat(t, carry):
        complete(t)
        work(t, "both")
        return carry

    lax.fori_loop(max(1, ahead), layers, treat, 0)

    sems = (back_layer_send, back_layer_recv, back_plane_send, back_plane_recv)
    back_layer, back_plane = exchange(
        sizes, lambda i: b_ref.at[i], lambda i: a_ref.at[i], beta_ref, alpha_ref, sems
    )
    keep = [
        pltpu.make_async_copy(b_ref.at[layer], beta_ref.at[layer], own_sem.at[5]),
        pltpu.make_async_copy(a_ref.at[me], alpha_ref.at[me], own_sem.at[6]),
    ]
    for copy in back_layer + back_plane + keep:
        copy.start()

    def finish(piece, upward):
        @pl.when(can_rise if upward else can_fall)
        def sent():
            relay(piece, upward).wait_send()

        for at in chips:
            to_chip(piece, at).wait_send()
        if square:
            to_corner(piece, 0).wait_send()
            to_corner(piece, 1).wait_send()
        if step == 2:
            for at in range(len(offsets)):
                to_pair(piece, at).wait_send()

    for k in range(1, layers):
        each_piece(k, finish)

    @pl.when(can_rise)
    def risen():
        relay(None, True).wait_send()

    @pl.when(can_fall)
    def fallen():
        relay(None, False).wait_send()

    for copy in back_plane + keep:
        copy.wait()

    def join(i):
        for p in range(rows * cols):
            at = pl.ds(pl.multiple_of(i * block, block), block)
            out_ref[at, p * block : (p + 1) * block] = beta_ref[i, p].T + alpha_ref[p, i]

    if wide:
        join(layer)
    for k, copy in enumerate(back_layer, 1):
        copy.wait()
        if wide:
            join(lax.rem(layer + layers - k, layers))


def wide_kernel(sizes, c, t, h, k, count, out_ref, columns, beta, alpha, *scratch):
    sigma_kernel(sizes, True, c, t, h, k, count, beta, alpha, columns, *scratch, out_ref=out_ref)


def local(sizes, coeffs, hblocks, hcount, hcols):
    rows, cols, layers = sizes
    group = rows * cols
    row_count, col_count = coeffs.shape
    share, block, _ = hblocks.shape
    stored = share * layers
    blocks = row_count * group // block
    alpha_rows, beta_rows = col_count // group, row_count // layers
    per_layer, per_plane = blocks // layers, blocks // group
    beta_back = (layers, per_layer, beta_rows, block)
    alpha_back = (group, per_plane, alpha_rows, block)
    f32 = jnp.float32
    dma = pltpu.SemaphoreType.DMA

    wide = alpha_rows == block and beta_rows == block
    names = hcols.reshape(1, share)
    if wide:
        for_layer, for_plane = coeffs, coeffs
        z_shape, x_shape = (layers, col_count, block), (group, row_count, block)
        y_shape, sum_shape = (blocks, 2 * block, 2 * block), (share + 1, block, 2 * block)
        held, turned = coeffs.shape, z_shape
    else:
        for_layer = coeffs.reshape(layers, beta_rows, col_count)
        for_plane = coeffs.T.reshape(group, alpha_rows, row_count)
        z_shape, x_shape = for_layer.shape, for_plane.shape
        both = alpha_rows + beta_rows
        y_shape, sum_shape = (blocks, both, 2 * block), (share + 1, both, block)
        held = turned = (8, 128)
    chips = group // 2 if cols % 2 == 0 else group
    smem = pl.BlockSpec(memory_space=pltpu.SMEM)
    gathered = jax.ShapeDtypeStruct((layers, *names.shape), jnp.int32)
    if wide:
        kernel = functools.partial(wide_kernel, sizes)
        out_shape = (jax.ShapeDtypeStruct((row_count, col_count), f32), gathered)
        out_specs = (pl.BlockSpec(memory_space=pltpu.VMEM), ANY)
        landing = [pltpu.VMEM(beta_back, f32), pltpu.VMEM(alpha_back, f32)]
    else:
        kernel = functools.partial(sigma_kernel, sizes, False)
        out_shape = (
            jax.ShapeDtypeStruct(beta_back, f32),
            jax.ShapeDtypeStruct(alpha_back, f32),
            gathered,
        )
        out_specs = (ANY,) * 3
        landing = []
    results = pl.pallas_call(
        kernel,
        out_shape=out_shape,
        in_specs=[ANY] * 4 + [smem],
        out_specs=out_specs,
        scratch_shapes=landing
        + [
            pltpu.VMEM(z_shape, f32),
            pltpu.VMEM(x_shape, f32),
            pltpu.VMEM((layers, share, block, block), f32),
            pltpu.VMEM(y_shape, jnp.bfloat16),
            pltpu.VMEM(sum_shape, f32),
            pltpu.VMEM(beta_back, f32),
            pltpu.VMEM(alpha_back, f32),
            pltpu.SMEM((layers, *names.shape), jnp.int32),
            pltpu.SMEM((stored,), f32),
            pltpu.VMEM(held, f32),
            pltpu.VMEM(turned, f32),
            dma((8,)),
        ]
        + ([dma((layers,))] * 2 + [dma((group,))] * 2) * 2
        + [dma((layers,))] * 5
        + [dma((layers, chips))] * 4,
        compiler_params=pltpu.CompilerParams(
            collective_id=0, has_side_effects=True, vmem_limit_bytes=56 * 2**20
        ),
        name="sigma",
    )(
        for_layer,
        for_plane,
        hblocks,
        names,
        hcount,
    )
    if wide:
        return results[0]
    beta, alpha, _ = results
    beta = beta.transpose(0, 2, 1, 3).reshape(row_count, col_count)
    alpha = alpha.transpose(1, 3, 0, 2).reshape(row_count, col_count)
    return beta + alpha


def solution(mesh):
    sizes = tuple(mesh.shape[name] for name in ("row", "col", "layer"))
    in_specs = (P(("row", "col"), "layer"), P("layer", None, None), P(), P("layer"))
    out_specs = P(("row", "col"), "layer")
    return jax.shard_map(
        functools.partial(local, sizes),
        mesh=mesh,
        in_specs=in_specs,
        out_specs=out_specs,
        check_vma=False,
    )
```
